32 devices in a mesh: groups: 2 (over y), leaf: 8 (over z, x), rhs: 2 (over core).
Axes of the slice: x: 2, y: 2, z: 4, core: 2. Of those that a mesh axis runs over, the one named last changes fastest.
Arguments:
- sources: bfloat16 [2, 192, 8192], P(None, None, ('groups', 'leaf', 'rhs')), parts along dimension 2, may hold values from -6 to 6
- forward_field: bfloat16 [2, 192, 8192], P(None, None, ('groups', 'leaf', 'rhs')), parts along dimension 2, may hold values from -6 to 6
- row_bases: bfloat16 [3, 2, 8192, 512], P(None, None, ('groups', 'leaf', 'rhs')), parts along dimension 2, may hold values from -0.09375 to 0.09375
- col_bases: bfloat16 [3, 2, 8192, 512], P(None, None, ('groups', 'leaf', 'rhs')), parts along dimension 2, may hold values from -0.1875 to 0.1875
- near_blocks: bfloat16 [2, 64, 8, 128, 128], P(None, ('groups', 'leaf', 'rhs')), parts along dimension 1, may hold values from -0.125 to 0.125
- near_index: int32 [64, 8], P(('groups', 'leaf', 'rhs')), parts along dimension 0, may hold values from 0 to 31, as said below
- cluster_order: int32 [8192], P(('groups', 'leaf', 'rhs')), parts along dimension 0, may hold values from 0 to 4095, as said below
Outputs:
- adjoint_field: float32 [2, 192, 8192], P(None, None, ('groups', 'leaf', 'rhs')), parts along dimension 2
- admittance_grad: float32 [8192], P(('groups', 'leaf', 'rhs')), parts along dimension 0
The draws below stay inside these ranges and needn't reach their ends.
There are 2 independent parts, one for each index of `groups`. The reference program is written for one: setup_inputs(seed, part) draws one part's arguments, and reference() takes and returns one part's arrays. A program takes and returns all parts, laid end to end along the dimension named above; each array names one. Nothing has to cross between parts.
Inputs may be any that keep to these rules, and one draw needn't show every extreme that they name: `near_index`: column 0 names the row's own block; every named block lies within 2 blocks of the row's own block. `cluster_order`: maps each aligned run of 256 tree positions (the panels of one device) onto the same run of panels, each panel once.
All inputs are finite; a program needn't handle non-finite values.
Results may differ from the reference program's by a relative error of at most 0.0023.
Values may be sent and summed in bfloat16 or wider, within the bound.
No kernel may reach another device: no remote copies, remote signals or barrier semaphores. Data moves between devices by JAX's collectives and lax.ppermute only.
A program may use at most 64 MiB of HBM per device.

```python
import math
import jax
import jax.numpy as jnp
from jax import lax

R = 192
RANK = 512
NB = 128
LEVELS = 3
K = 8
PAN_DEV = 256
NPAN = 4096
NBLK = 32
NB_DEV = 2


def draw_cluster_order(key, part):
    key = jax.random.fold_in(key, 11)
    scores = jax.random.randint(key, (NPAN,), 0, 1 << 18)
    scores = scores * PAN_DEV + jnp.arange(NPAN, dtype=jnp.int32) % PAN_DEV
    ranked = jnp.argsort(scores.reshape(-1, PAN_DEV), axis=1).astype(jnp.int32)
    starts = (jnp.arange(NPAN // PAN_DEV, dtype=jnp.int32) * PAN_DEV)[:, None]
    return (ranked + starts).reshape(-1).astype(jnp.int32)


def draw_near_index(key, part):
    key = jax.random.fold_in(key, 12)
    offsets = jax.random.randint(key, (NBLK, K - 1), -NB_DEV, NB_DEV + 1)
    row_ids = jnp.arange(NBLK, dtype=jnp.int32)[:, None]
    targets = jnp.clip(row_ids + offsets, 0, NBLK - 1)
    return jnp.concatenate([row_ids, targets], axis=1).astype(jnp.int32)


def steps_of(rng, extent, pieces, smallest, largest):
    def one(axis_at, shards_of):
        steps = jax.random.uniform(jax.random.fold_in(jax.random.fold_in(rng, 6), axis_at), (shards_of,), jnp.float32, smallest / len(pieces), largest / len(pieces))
        return jnp.repeat(jnp.exp(steps), extent[axis_at] // shards_of).reshape((-1,) + (1,) * (len(extent) - axis_at - 1))

    factor_of = one(*pieces[0])
    for cut in pieces[1:]:
        factor_of = factor_of * one(*cut)
    return factor_of


def centred(key, shape, scale, most, split=(), kind=jnp.bfloat16):
    array = jax.random.normal(key, shape, jnp.float32) * scale
    if len(split) > 0:
        array = steps_of(key, shape, split, -0.22, 0.18) * array
    return jnp.clip(array, min=-most, max=most).astype(kind)


def setup_inputs(seed: int = 0, part: int = 0) -> dict:
    key_list = jax.random.split(jax.random.key(seed), 8)
    part_keys = jax.random.split(jax.random.fold_in(key_list[7], part), 8)
    return {
        "sources": centred(part_keys[0], (2, R, NPAN), 1.0, 6.0, ((2, 16),)),
        "forward_field": centred(part_keys[1], (2, R, NPAN), 1.0, 6.0, ((2, 16),)),
        "row_bases": centred(part_keys[2], (LEVELS, 2, NPAN, RANK), NPAN ** -0.5, 0.09375, ((2, 16),)),
        "col_bases": centred(part_keys[3], (LEVELS, 2, NPAN, RANK), (2 * RANK) ** -0.5, 0.1875, ((2, 16),)),
        "near_blocks": centred(part_keys[4], (2, NBLK, K, NB, NB), (2 * K * NB) ** -0.5, 0.125, ((1, 16),)),
        "near_index": draw_near_index(jax.random.fold_in(jax.random.fold_in(key_list[7], part), 71), part),
        "cluster_order": draw_cluster_order(jax.random.fold_in(jax.random.fold_in(key_list[7], part), 71), part),
    }


def conj_product(first_operand, second_operand, pattern):
    highest = lax.Precision.HIGHEST
    real_part = jnp.einsum(pattern, first_operand[0], second_operand[0], precision=highest) + jnp.einsum(pattern, first_operand[1], second_operand[1], precision=highest)
    imag_part = jnp.einsum(pattern, first_operand[1], second_operand[0], precision=highest) - jnp.einsum(pattern, first_operand[0], second_operand[1], precision=highest)
    return jnp.stack([real_part, imag_part])

def plain_product(first_operand, second_operand, pattern):
    highest = lax.Precision.HIGHEST
    real_part = jnp.einsum(pattern, first_operand[0], second_operand[0], precision=highest) - jnp.einsum(pattern, first_operand[1], second_operand[1], precision=highest)
    imag_part = jnp.einsum(pattern, first_operand[0], second_operand[1], precision=highest) + jnp.einsum(pattern, first_operand[1], second_operand[0], precision=highest)
    return jnp.stack([real_part, imag_part])

def reference(sources, forward_field, row_bases, col_bases, near_blocks, near_index, cluster_order):
    tree_sources = sources[:, :, cluster_order].astype(jnp.float32)
    block_sources = tree_sources.reshape(2, R, NBLK, NB)
    near_float = near_blocks.astype(jnp.float32)
    contributions = conj_product(block_sources, near_float, 'rib,ikbc->rikc')
    flat_terms = jnp.transpose(contributions, (2, 3, 0, 1, 4)).reshape(NBLK * K, 2, R, NB)
    block_sums = jax.ops.segment_sum(flat_terms, near_index.reshape(-1), num_segments=NBLK)
    adjoint_tree = jnp.transpose(block_sums, (1, 2, 0, 3)).reshape(2, R, NPAN)
    for level_number in range(1, LEVELS + 1):
        node_count = 2 ** level_number
        node_size = NPAN // node_count
        node_sources = tree_sources.reshape(2, R, node_count, node_size)
        row_basis = row_bases[level_number - 1].astype(jnp.float32).reshape(2, node_count, node_size, RANK)
        coefficients = conj_product(node_sources, row_basis, 'rsn,snk->rsk')
        coefficients = lax.optimization_barrier(coefficients.astype(jnp.bfloat16)).astype(jnp.float32)
        coefficients = coefficients.reshape(2, R, node_count // 2, 2, RANK)[:, :, :, ::-1, :].reshape(2, R, node_count, RANK)
        col_basis = col_bases[level_number - 1].astype(jnp.float32).reshape(2, node_count, node_size, RANK)
        adjoint_tree = adjoint_tree + plain_product(coefficients, col_basis, 'rsk,snk->rsn').reshape(2, R, NPAN)
    adjoint_field = jnp.zeros((2, R, NPAN), jnp.float32).at[:, :, cluster_order].set(adjoint_tree)
    forward_float = forward_field.astype(jnp.float32)
    gradient = -lax.optimization_barrier(jnp.sum(adjoint_field * forward_float, axis=(0, 1))) / math.sqrt(R)
    return (adjoint_field, gradient)
```

```python
import math

import jax
import jax.numpy as jnp
from jax import lax
from jax.experimental import pallas as pl
from jax.experimental.pallas import tpu as pltpu
from jax.sharding import PartitionSpec as P

TREE = ("leaf", "rhs")
F32 = jnp.float32
BF16 = jnp.bfloat16
VMEM_BYTES = 24 * 1024 * 1024


def dot(a, b):
    return lax.dot_general(a, b, (((1,), (0,)), ((), ())), preferred_element_type=F32)


def dot_t(a, b):
    return lax.dot_general(a, b, (((1,), (1,)), ((), ())), preferred_element_type=F32)


def call(kernel, out_shape, scratch_shapes=(), smem=(), inputs=0):
    in_specs = [
        pl.BlockSpec(memory_space=pltpu.SMEM if i in smem else pltpu.VMEM) for i in range(inputs)
    ]
    out_specs = jax.tree.map(lambda _: pl.BlockSpec(memory_space=pltpu.VMEM), out_shape)
    return pl.pallas_call(
        kernel,
        out_shape=out_shape,
        in_specs=in_specs,
        out_specs=out_specs,
        scratch_shapes=list(scratch_shapes),
        compiler_params=pltpu.CompilerParams(vmem_limit_bytes=VMEM_BYTES),
    )


def array(shape, dtype):
    return jax.ShapeDtypeStruct(shape, dtype)


def swapped(x, distance):
    return lax.ppermute(x, TREE, [(i, i ^ distance) for i in range(lax.axis_size(TREE))])


def by_core(x, distance_0, distance_1):
    pairs = []
    for i in range(lax.axis_size(TREE)):
        distance = distance_1 if i & 1 else distance_0
        if distance is not None:
            pairs.append((i, i ^ distance))
    return lax.ppermute(x, TREE, pairs)


def one_hot_of(order_ref, panels):
    local = lax.rem(order_ref[...], panels)
    rows = lax.broadcasted_iota(jnp.int32, (panels, panels), 0)
    return (rows == local).astype(F32).astype(BF16)


def signed_stack(x):
    half = x.shape[0] // 2
    real, imag = x[:half], x[half:]
    return jnp.concatenate(
        [jnp.concatenate([real, imag], axis=1), jnp.concatenate([imag, -real], axis=1)], axis=0
    )


def position():
    place = lax.axis_index(TREE)
    return place & 1, (place >> 1) & 1, (place >> 2) & 1


def first_kernel(order_ref, src_ref, basis_ref, tree_ref, send_ref, keep_ref):
    core, _, low = position()
    two, rows, panels = src_ref.shape
    rank = basis_ref.shape[3]
    half = rank // 2
    source = src_ref[...].reshape(two * rows, panels)
    tree = dot(source, one_hot_of(order_ref, panels)).astype(BF16)
    tree_ref[...] = tree
    stack = signed_stack(tree)
    mine = pl.multiple_of((low ^ core) * half, half)
    theirs = pl.multiple_of((low ^ core ^ 1) * half, half)
    for start, out in ((theirs, send_ref), (mine, keep_ref)):
        basis = basis_ref[0, :, :, pl.ds(start, half)].reshape(2 * panels, half)
        out[...] = dot(stack, basis)


def second_kernel(tree_ref, basis_ref, send_ref, keep_ref):
    core, _, _ = position()
    levels, _, panels, rank = basis_ref.shape
    half = rank // 2
    stack = signed_stack(tree_ref[...])
    mine = pl.multiple_of(core * half, half)
    theirs = pl.multiple_of((core ^ 1) * half, half)
    for start, out in ((theirs, send_ref), (mine, keep_ref)):
        for level in range(1, levels):
            basis = basis_ref[level, :, :, pl.ds(start, half)].reshape(2 * panels, half)
            out[level - 1] = dot(stack, basis)


def near_kernel(index_ref, tree_ref, near_ref, core_ref, far_ref, own_ref, sums):
    core, _, _ = position()
    _, block_count, neighbours, size, _ = near_ref.shape
    sums[...] = jnp.zeros_like(sums)
    base = index_ref[0, 0] - block_count
    for i in range(block_count):
        stack = signed_stack(tree_ref[:, i * size : (i + 1) * size])
        for k in range(neighbours):
            block = near_ref[:, i, k].reshape(2 * size, size)
            target = jnp.clip(index_ref[i, k] - base, 0, 3 * block_count - 1)
            sums[target] += dot(stack, block)
    for j in range(block_count):
        lanes = pl.ds(j * size, size)
        own_ref[:, lanes] = sums[block_count + j]
        far_ref[:, lanes] = sums[core * 2 * block_count + j].astype(BF16)
        core_ref[:, lanes] = sums[(1 - core) * 2 * block_count + j]


def spread_kernel(keep_ref, got_ref, out_ref, other_ref):
    core, across, _ = position()
    width = out_ref.shape[1]
    out_lanes = pl.ds(pl.multiple_of((across ^ 1 ^ core) * width, width), width)
    other_lanes = pl.ds(pl.multiple_of((across ^ core) * width, width), width)
    out_ref[...] = keep_ref[:, out_lanes] + got_ref[:, out_lanes]
    other_ref[...] = keep_ref[:, other_lanes] + got_ref[:, other_lanes]


def expanded(coefficient, basis_ref, level, start, width):
    half = coefficient.shape[0] // 2
    turned = jnp.concatenate([-coefficient[half:], coefficient[:half]], axis=0)
    lanes = pl.ds(start, width)
    return dot_t(coefficient, basis_ref[level, 0, :, lanes]) + dot_t(
        turned, basis_ref[level, 1, :, lanes]
    )


def middle_kernel(own_ref, core_ref, far_ref, two_ref, two_got_ref, three_ref, three_got_ref, basis_ref, out_ref):
    core, _, _ = position()
    half = two_ref.shape[1]
    total = own_ref[...] + core_ref[...] + far_ref[...].astype(F32)
    for level, mine_ref, got_ref in ((1, two_ref, two_got_ref), (2, three_ref, three_got_ref)):
        total += expanded(mine_ref[...], basis_ref, level, pl.multiple_of(core * half, half), half)
        total += expanded(got_ref[...], basis_ref, level, pl.multiple_of((1 - core) * half, half), half)
    out_ref[...] = total


def last_kernel(
    order_ref, base_ref, f_ref, g_ref, f_got_ref, g_got_ref, basis_ref, forward_ref, field_ref, grad_ref, full
):
    core, across, low = position()
    width = f_ref.shape[1]
    mine = low ^ core
    for half, first, second in ((mine, f_ref, g_ref), (mine ^ 1, f_got_ref, g_got_ref)):
        full[:, pl.ds(pl.multiple_of((2 * half + across) * width, width), width)] = first[...]
        full[:, pl.ds(pl.multiple_of((2 * half + (across ^ 1)) * width, width), width)] = second[...]
    total = base_ref[...] + expanded(full[...], basis_ref, 0, 0, 4 * width)
    two, rows, panels = field_ref.shape
    one_hot = one_hot_of(order_ref, panels)
    field = jnp.zeros_like(total)
    for _ in range(3):
        piece = total.astype(BF16)
        total = total - piece.astype(F32)
        field += dot_t(piece, one_hot)
    field_ref[...] = field.reshape(two, rows, panels)
    forward = forward_ref[...].reshape(two * rows, panels).astype(F32)
    grad_ref[...] = -jnp.sum(field * forward, axis=0, keepdims=True) / math.sqrt(rows)


def fast_body(sources, forward_field, row_bases, col_bases, near_blocks, near_index, cluster_order):
    two, rows, panels = sources.shape
    rank = row_bases.shape[3]
    both = two * rows
    half, quarter = rank // 2, rank // 4
    order = cluster_order.reshape(1, panels)
    core = lax.axis_index(TREE) & 1

    tree, send_1, keep_1 = call(
        first_kernel,
        (array((both, panels), BF16), array((both, half), F32), array((both, half), F32)),
        inputs=3,
    )(order, sources, row_bases)
    got_1 = swapped(send_1, 1)
    send_23, keep_23 = call(
        second_kernel, (array((2, both, half), F32), array((2, both, half), F32)), inputs=2
    )(tree, row_bases)
    got_23 = swapped(send_23, 1)

    to_a, other = call(
        spread_kernel, (array((both, quarter), F32), array((both, quarter), F32)), inputs=2
    )(keep_1, got_1)
    got_a = by_core(to_a, 2, 4)
    got_b = by_core(other, None, 6)

    sum_23 = keep_23 + got_23
    mine_3 = swapped(sum_23[1].astype(BF16), 2)
    two_sent = sum_23[0].astype(BF16)
    got_c = swapped(two_sent, 4)
    got_d = swapped(two_sent, 6)

    blocks = near_blocks.shape[1]
    size = near_blocks.shape[3]
    to_core, to_far, own = call(
        near_kernel,
        (array((both, panels), F32), array((both, panels), BF16), array((both, panels), F32)),
        scratch_shapes=[pltpu.VMEM((3 * blocks, both, size), F32)],
        smem=(0,),
        inputs=3,
    )(near_index, tree, near_blocks)
    core_halo = swapped(to_core, 1)
    peers = lax.axis_size(TREE)
    joints = [(i, i + 1) for i in range(1, peers - 1, 2)]
    far_halo = lax.ppermute(to_far, TREE, joints + [(b, a) for a, b in joints])

    middle = got_a + jnp.where(core == 0, other, got_b)
    quarter_sum = (middle + swapped(middle, 1)).astype(BF16)
    got_f = by_core(quarter_sum, 8, 12)
    got_g = by_core(quarter_sum, 10, 14)

    mine_2 = (got_c.astype(F32) + got_d.astype(F32)).astype(BF16)
    other_3 = swapped(mine_3, 1)
    other_2 = swapped(mine_2, 1)
    base = call(middle_kernel, array((both, panels), F32), inputs=8)(
        own, core_halo, far_halo, mine_2, other_2, mine_3, other_3, col_bases
    )
    core_f = swapped(got_f, 1)
    core_g = swapped(got_g, 1)
    field, grad = call(
        last_kernel,
        (array((two, rows, panels), F32), array((1, panels), F32)),
        scratch_shapes=[pltpu.VMEM((both, rank), BF16)],
        inputs=8,
    )(order, base, got_f, got_g, core_f, core_g, col_bases, forward_field)
    return field, grad.reshape(panels)


def conj_product(first_operand, second_operand, pattern):
    real_part = jnp.einsum(
        pattern, first_operand[0], second_operand[0], preferred_element_type=jnp.float32
    ) + jnp.einsum(pattern, first_operand[1], second_operand[1], preferred_element_type=jnp.float32)
    imag_part = jnp.einsum(
        pattern, first_operand[1], second_operand[0], preferred_element_type=jnp.float32
    ) - jnp.einsum(pattern, first_operand[0], second_operand[1], preferred_element_type=jnp.float32)
    return jnp.stack([real_part, imag_part])


def expand_basis(coefficient, col_basis):
    real_part = jnp.einsum(
        "rk,nk->rn", coefficient[0], col_basis[0], preferred_element_type=jnp.float32
    ) - jnp.einsum("rk,nk->rn", coefficient[1], col_basis[1], preferred_element_type=jnp.float32)
    imag_part = jnp.einsum(
        "rk,nk->rn", coefficient[0], col_basis[1], preferred_element_type=jnp.float32
    ) + jnp.einsum("rk,nk->rn", coefficient[1], col_basis[0], preferred_element_type=jnp.float32)
    return jnp.stack([real_part, imag_part])


def from_behind(x, by):
    peers = lax.axis_size(TREE)
    return lax.ppermute(x, TREE, [(i, i + by) for i in range(peers) if 0 <= i + by < peers])


def general_body(sources, forward_field, row_bases, col_bases, near_blocks, near_index, cluster_order):
    panel_count = sources.shape[2]
    columns = sources.shape[1]
    device = lax.axis_index(TREE)
    tree_bits = lax.axis_size(TREE).bit_length() - 1
    level_total = row_bases.shape[0]
    local_order = cluster_order - device * panel_count
    tree_sources = jnp.take(sources, local_order, axis=2)
    partials = [
        conj_product(tree_sources, row_bases[level_number], "rn,nk->rk")
        for level_number in range(level_total)
    ]
    block_count = near_blocks.shape[1]
    block_size = near_blocks.shape[3]
    targets = near_index - device * block_count + block_count
    one_hot = (
        targets[:, :, None] == jnp.arange(3 * block_count, dtype=jnp.int32)[None, None, :]
    ).astype(jnp.float32)
    block_sources = tree_sources.reshape(2, columns, block_count, block_size)
    terms = conj_product(block_sources, near_blocks, "rib,ikbc->rikc")
    buffer = jnp.einsum("zrikc,ikj->zrjc", terms, one_hot, precision=lax.Precision.HIGHEST)
    from_right = from_behind(buffer[:, :, :block_count], -1)
    from_left = from_behind(buffer[:, :, 2 * block_count :], 1)
    near_field = buffer[:, :, block_count : 2 * block_count] + from_right + from_left
    adjoint_tree = near_field.reshape(2, columns, panel_count)
    level_sums = []
    for level_number in range(level_total):
        running = partials[level_number]
        for bit_number in range(tree_bits - level_number - 1):
            running = running + swapped(running, 1 << bit_number)
        level_sums.append(running.astype(jnp.bfloat16))
    for level_number in range(level_total):
        sibling = swapped(level_sums[level_number], 1 << (tree_bits - level_number - 1))
        adjoint_tree = adjoint_tree + expand_basis(sibling, col_bases[level_number])
    adjoint_field = (
        jnp.zeros((2, columns, panel_count), jnp.float32).at[:, :, local_order].set(adjoint_tree)
    )
    forward_float = forward_field.astype(jnp.float32)
    gradient = -jnp.sum(adjoint_field * forward_float, axis=(0, 1)) / math.sqrt(columns)
    return (adjoint_field, gradient)


def body(*arrays):
    row_bases = arrays[2]
    fits = lax.axis_size("rhs") == 2 and lax.axis_size("leaf") == 8 and row_bases.shape[0] == 3
    return (fast_body if fits else general_body)(*arrays)


def solution(mesh):
    split = ("groups", "leaf", "rhs")
    in_specs = (
        P(None, None, split),
        P(None, None, split),
        P(None, None, split, None),
        P(None, None, split, None),
        P(None, split, None, None, None),
        P(split, None),
        P(split),
    )
    out_specs = (P(None, None, split), P(split))
    return jax.shard_map(body, mesh=mesh, in_specs=in_specs, out_specs=out_specs, check_vma=False)
```

```python
import math

import jax
import jax.numpy as jnp
from jax import lax
from jax.experimental import pallas as pl
from jax.experimental.pallas import tpu as pltpu
from jax.sharding import PartitionSpec as P

TREE = ("leaf", "rhs")
F32 = jnp.float32
BF16 = jnp.bfloat16
VMEM_BYTES = 12 * 1024 * 1024


def dot(a, b):
    return lax.dot_general(a, b, (((1,), (0,)), ((), ())), preferred_element_type=F32)


def dot_t(a, b):
    return lax.dot_general(a, b, (((1,), (1,)), ((), ())), preferred_element_type=F32)


def call(kernel, out_shape, inputs, scratch_shapes=(), smem=(), far=(), vmem=VMEM_BYTES):
    def place(i):
        if i in far:
            return pl.BlockSpec(memory_space=pltpu.HBM)
        return pl.BlockSpec(memory_space=pltpu.SMEM if i in smem else pltpu.VMEM)

    return pl.pallas_call(
        kernel,
        out_shape=out_shape,
        in_specs=[place(i) for i in range(inputs)],
        out_specs=jax.tree.map(lambda _: pl.BlockSpec(memory_space=pltpu.VMEM), out_shape),
        scratch_shapes=list(scratch_shapes),
        compiler_params=pltpu.CompilerParams(vmem_limit_bytes=vmem),
    )


def array(shape, dtype):
    return jax.ShapeDtypeStruct(shape, dtype)


def swapped(x, distance):
    return lax.ppermute(x, TREE, [(i, i ^ distance) for i in range(lax.axis_size(TREE))])


def by_core(x, distance_0, distance_1):
    pairs = []
    for i in range(lax.axis_size(TREE)):
        distance = distance_1 if i & 1 else distance_0
        if distance is not None:
            pairs.append((i, i ^ distance))
    return lax.ppermute(x, TREE, pairs)


def after(x, *others):
    return lax.optimization_barrier((x, *others))[0]


EXTRA = 16
TOP = 14.0


def scaled_to(out_ref, values):
    rows = values.shape[0]
    largest = jnp.max(jnp.max(jnp.abs(values), axis=0, keepdims=True), axis=1, keepdims=True)
    power = jnp.clip(jnp.ceil(jnp.log2(jnp.maximum(largest, 1e-30))), -100.0, 100.0)
    out_ref[:rows] = values * jnp.exp2(TOP - power)
    out_ref[rows:] = jnp.broadcast_to(power, (EXTRA, values.shape[1]))


def unscaled(packed):
    packed = packed.astype(F32)
    rows = packed.shape[0] - EXTRA
    return packed[:rows] * jnp.exp2(packed[rows : rows + 1] - TOP)


def one_hot_of(order_ref, panels):
    local = lax.rem(order_ref[...], panels)
    rows = lax.broadcasted_iota(jnp.int32, (panels, panels), 0)
    return (rows == local).astype(F32).astype(BF16)


def signed_stack(x):
    half = x.shape[0] // 2
    real, imag = x[:half], x[half:]
    return jnp.concatenate(
        [jnp.concatenate([real, imag], axis=1), jnp.concatenate([imag, -real], axis=1)], axis=0
    )


def position():
    place = lax.axis_index(TREE)
    return place & 1, (place >> 1) & 1, (place >> 2) & 1


def first_kernel(
    order_hbm,
    src_hbm,
    basis_hbm,
    tree_ref,
    send_1_ref,
    keep_1_ref,
    part_2_ref,
    send_3_ref,
    keep_3_ref,
    order,
    source,
    basis,
    sems,
):
    core, _, low = position()
    two, rows, panels = source.shape
    rank = basis.shape[3]
    half = rank // 2
    copies = [
        pltpu.make_async_copy(order_hbm, order, sems.at[0]),
        pltpu.make_async_copy(src_hbm, source, sems.at[1]),
    ] + [
        pltpu.make_async_copy(basis_hbm.at[level], basis.at[level], sems.at[2 + level])
        for level in range(3)
    ]
    for copy in copies:
        copy.start()
    copies[0].wait()
    one_hot = one_hot_of(order, panels)
    copies[1].wait()
    tree = dot(source[...].reshape(two * rows, panels), one_hot).astype(BF16)
    tree_ref[...] = tree
    stack = signed_stack(tree)

    def product(level, start, width):
        columns = basis[level, :, :, pl.ds(start, width)].reshape(2 * panels, width)
        return dot(stack, columns)

    copies[2].wait()
    send_1_ref[...] = product(0, pl.multiple_of((low ^ core ^ 1) * half, half), half)
    keep_1_ref[...] = product(0, pl.multiple_of((low ^ core) * half, half), half)
    copies[3].wait()
    part_2_ref[...] = product(1, 0, rank)
    copies[4].wait()
    send_3_ref[...] = product(2, pl.multiple_of((core ^ 1) * half, half), half)
    keep_3_ref[...] = product(2, pl.multiple_of(core * half, half), half)


def near_kernel(index_ref, tree_ref, near_ref, core_ref, far_ref, own_ref, sums):
    core, _, _ = position()
    _, block_count, neighbours, size, _ = near_ref.shape
    sums[...] = jnp.zeros_like(sums)
    base = index_ref[0, 0] - block_count
    for i in range(block_count):
        stack = signed_stack(tree_ref[:, i * size : (i + 1) * size])
        for k in range(neighbours):
            block = near_ref[:, i, k].reshape(2 * size, size)
            target = jnp.clip(index_ref[i, k] - base, 0, 3 * block_count - 1)
            sums[target] += dot(stack, block)
    for j in range(block_count):
        lanes = pl.ds(j * size, size)
        own_ref[:, lanes] = sums[block_count + j]
        far_ref[:, lanes] = sums[core * 2 * block_count + j].astype(BF16)
        core_ref[:, lanes] = sums[(1 - core) * 2 * block_count + j].astype(BF16)


def spread_kernel(keep_ref, got_ref, out_ref, other_ref):
    core, across, _ = position()
    width = out_ref.shape[1]
    out_lanes = pl.ds(pl.multiple_of((across ^ 1 ^ core) * width, width), width)
    other_lanes = pl.ds(pl.multiple_of((across ^ core) * width, width), width)
    out_ref[...] = keep_ref[:, out_lanes] + got_ref[:, out_lanes]
    other_ref[...] = keep_ref[:, other_lanes] + got_ref[:, other_lanes]


def sums_kernel(part_2_ref, got_2_ref, keep_3_ref, got_3_ref, two_ref, three_ref):
    three_ref[...] = (keep_3_ref[...] + got_3_ref[...]).astype(BF16)
    scaled_to(two_ref, part_2_ref[...] + got_2_ref[...])


def expanded(coefficient, basis_ref, level, start, width):
    half = coefficient.shape[0] // 2
    turned = jnp.concatenate([-coefficient[half:], coefficient[:half]], axis=0)
    lanes = pl.ds(start, width)
    return dot_t(coefficient, basis_ref[level, 0, :, lanes]) + dot_t(
        turned, basis_ref[level, 1, :, lanes]
    )


def halo_kernel(own_ref, far_ref, three_ref, pair_ref, basis_ref, out_ref):
    core, _, _ = position()
    rows, half = three_ref.shape
    total = own_ref[...] + far_ref[...].astype(F32) + pair_ref[rows:].astype(F32)
    total += expanded(three_ref[...], basis_ref, 2, pl.multiple_of(core * half, half), half)
    total += expanded(pair_ref[:rows], basis_ref, 2, pl.multiple_of((1 - core) * half, half), half)
    out_ref[...] = total


def second_kernel(base_ref, two_ref, basis_ref, out_ref):
    out_ref[...] = base_ref[...] + expanded(two_ref[...], basis_ref, 1, 0, two_ref.shape[1])


def last_kernel(
    order_ref, base_ref, mine_ref, got_ref, basis_ref, forward_ref, field_ref, grad_ref, full
):
    core, across, low = position()
    both = base_ref.shape[0]
    width = mine_ref.shape[1]
    mine = low ^ core
    for half, part in ((mine, mine_ref), (mine ^ 1, got_ref)):
        full[:, pl.ds(pl.multiple_of((2 * half + across) * width, width), width)] = part[:both]
        full[:, pl.ds(pl.multiple_of((2 * half + (across ^ 1)) * width, width), width)] = part[both:]
    total = base_ref[...] + expanded(full[...], basis_ref, 0, 0, 4 * width)
    two, rows, panels = field_ref.shape
    one_hot = one_hot_of(order_ref, panels)
    field = jnp.zeros_like(total)
    for _ in range(3):
        piece = total.astype(BF16)
        total = total - piece.astype(F32)
        field += dot_t(piece, one_hot)
    field_ref[...] = field.reshape(two, rows, panels)
    forward = forward_ref[...].reshape(two * rows, panels).astype(F32)
    grad_ref[...] = -jnp.sum(field * forward, axis=0, keepdims=True) / math.sqrt(rows)


def fast_body(sources, forward_field, row_bases, col_bases, near_blocks, near_index, cluster_order):
    two, rows, panels = sources.shape
    rank = row_bases.shape[3]
    both = two * rows
    half, quarter = rank // 2, rank // 4
    order = cluster_order.reshape(1, panels)
    core = lax.axis_index(TREE) & 1
    halves = array((both, half), F32)

    tree, send_1, keep_1, part_2, send_3, keep_3 = call(
        first_kernel,
        (array((both, panels), BF16), halves, halves, array((both, rank), F32), halves, halves),
        3,
        scratch_shapes=[
            pltpu.VMEM((1, panels), jnp.int32),
            pltpu.VMEM((two, rows, panels), BF16),
            pltpu.VMEM((3, 2, panels, rank), BF16),
            pltpu.SemaphoreType.DMA((5,)),
        ],
        far=(0, 1, 2),
        vmem=56 * 1024 * 1024,
    )(order, sources, row_bases)
    got_1 = swapped(send_1, 1)
    got_3 = swapped(send_3, 1)
    got_2 = swapped(part_2, 1)

    blocks = near_blocks.shape[1]
    size = near_blocks.shape[3]
    to_core, to_far, own = call(
        near_kernel,
        (array((both, panels), BF16), array((both, panels), BF16), array((both, panels), F32)),
        3,
        scratch_shapes=[pltpu.VMEM((3 * blocks, both, size), F32)],
        smem=(0,),
    )(near_index, tree, near_blocks)

    got_1, own = lax.optimization_barrier((got_1, own))
    to_a, to_b = call(
        spread_kernel, (array((both, quarter), F32), array((both, quarter), F32)), 2
    )(keep_1, got_1)
    got_a = by_core(to_a, 2, 4)
    got_b = by_core(to_b, None, 6)

    two_sent, three_sent = call(
        sums_kernel, (array((both + EXTRA, rank), F32), array((both, half), BF16)), 4
    )(part_2, got_2, keep_3, after(got_3, to_a))
    mine_3 = swapped(three_sent, 2)
    two_sent = two_sent.astype(jnp.float16)
    got_cd = by_core(two_sent, 4, 6)
    peers = lax.axis_size(TREE)
    joints = [(i, i + 1) for i in range(1, peers - 1, 2)]
    far_halo = lax.ppermute(after(to_far, to_a), TREE, joints + [(b, a) for a, b in joints])

    got_a, got_b, _ = lax.optimization_barrier((got_a, got_b, two_sent))
    middle = got_a + jnp.where(core == 0, to_b, got_b)
    parts = lax.all_gather(middle, "rhs", axis=0)
    quarter_sum = (parts[0] + parts[1]).astype(BF16)
    got_f = by_core(quarter_sum, 8, 12)
    got_g = by_core(quarter_sum, 10, 14)

    mine_3, own, _ = lax.optimization_barrier((mine_3, own, quarter_sum))
    pair_3 = swapped(jnp.concatenate([mine_3, to_core], axis=0), 1)
    base = call(halo_kernel, array((both, panels), F32), 5)(own, far_halo, mine_3, pair_3, col_bases)
    got_cd = after(got_cd, quarter_sum)
    all_2 = (unscaled(got_cd) + unscaled(swapped(got_cd, 1))).astype(BF16)
    base = call(second_kernel, array((both, panels), F32), 3)(base, all_2, col_bases)
    mine_1 = jnp.concatenate([got_f, got_g], axis=0)
    field, grad = call(
        last_kernel,
        (array((two, rows, panels), F32), array((1, panels), F32)),
        6,
        scratch_shapes=[pltpu.VMEM((both, rank), BF16)],
    )(order, base, mine_1, swapped(mine_1, 1), col_bases, forward_field)
    return field, grad.reshape(panels)


def conj_product(first_operand, second_operand, pattern):
    real_part = jnp.einsum(
        pattern, first_operand[0], second_operand[0], preferred_element_type=jnp.float32
    ) + jnp.einsum(pattern, first_operand[1], second_operand[1], preferred_element_type=jnp.float32)
    imag_part = jnp.einsum(
        pattern, first_operand[1], second_operand[0], preferred_element_type=jnp.float32
    ) - jnp.einsum(pattern, first_operand[0], second_operand[1], preferred_element_type=jnp.float32)
    return jnp.stack([real_part, imag_part])


def expand_basis(coefficient, col_basis):
    real_part = jnp.einsum(
        "rk,nk->rn", coefficient[0], col_basis[0], preferred_element_type=jnp.float32
    ) - jnp.einsum("rk,nk->rn", coefficient[1], col_basis[1], preferred_element_type=jnp.float32)
    imag_part = jnp.einsum(
        "rk,nk->rn", coefficient[0], col_basis[1], preferred_element_type=jnp.float32
    ) + jnp.einsum("rk,nk->rn", coefficient[1], col_basis[0], preferred_element_type=jnp.float32)
    return jnp.stack([real_part, imag_part])


def from_behind(x, by):
    peers = lax.axis_size(TREE)
    return lax.ppermute(x, TREE, [(i, i + by) for i in range(peers) if 0 <= i + by < peers])


def general_body(sources, forward_field, row_bases, col_bases, near_blocks, near_index, cluster_order):
    panel_count = sources.shape[2]
    columns = sources.shape[1]
    device = lax.axis_index(TREE)
    tree_bits = lax.axis_size(TREE).bit_length() - 1
    level_total = row_bases.shape[0]
    local_order = cluster_order - device * panel_count
    tree_sources = jnp.take(sources, local_order, axis=2)
    partials = [
        conj_product(tree_sources, row_bases[level_number], "rn,nk->rk")
        for level_number in range(level_total)
    ]
    block_count = near_blocks.shape[1]
    block_size = near_blocks.shape[3]
    targets = near_index - device * block_count + block_count
    one_hot = (
        targets[:, :, None] == jnp.arange(3 * block_count, dtype=jnp.int32)[None, None, :]
    ).astype(jnp.float32)
    block_sources = tree_sources.reshape(2, columns, block_count, block_size)
    terms = conj_product(block_sources, near_blocks, "rib,ikbc->rikc")
    buffer = jnp.einsum("zrikc,ikj->zrjc", terms, one_hot, precision=lax.Precision.HIGHEST)
    from_right = from_behind(buffer[:, :, :block_count], -1)
    from_left = from_behind(buffer[:, :, 2 * block_count :], 1)
    near_field = buffer[:, :, block_count : 2 * block_count] + from_right + from_left
    adjoint_tree = near_field.reshape(2, columns, panel_count)
    level_sums = []
    for level_number in range(level_total):
        running = partials[level_number]
        for bit_number in range(tree_bits - level_number - 1):
            running = running + swapped(running, 1 << bit_number)
        level_sums.append(running.astype(jnp.bfloat16))
    for level_number in range(level_total):
        sibling = swapped(level_sums[level_number], 1 << (tree_bits - level_number - 1))
        adjoint_tree = adjoint_tree + expand_basis(sibling, col_bases[level_number])
    adjoint_field = (
        jnp.zeros((2, columns, panel_count), jnp.float32).at[:, :, local_order].set(adjoint_tree)
    )
    forward_float = forward_field.astype(jnp.float32)
    gradient = -jnp.sum(adjoint_field * forward_float, axis=(0, 1)) / math.sqrt(columns)
    return (adjoint_field, gradient)


def body(*arrays):
    row_bases = arrays[2]
    fits = lax.axis_size("rhs") == 2 and lax.axis_size("leaf") == 8 and row_bases.shape[0] == 3
    return (fast_body if fits else general_body)(*arrays)


def solution(mesh):
    split = ("groups", "leaf", "rhs")
    in_specs = (
        P(None, None, split),
        P(None, None, split),
        P(None, None, split, None),
        P(None, None, split, None),
        P(None, split, None, None, None),
        P(split, None),
        P(split),
    )
    out_specs = (P(None, None, split), P(split))
    return jax.shard_map(body, mesh=mesh, in_specs=in_specs, out_specs=out_specs, check_vma=False)
```

```python
import math

import jax
import jax.numpy as jnp
from jax import lax
from jax.experimental import pallas as pl
from jax.experimental.pallas import tpu as pltpu
from jax.sharding import PartitionSpec as P

TREE = ("leaf", "rhs")
F32 = jnp.float32
BF16 = jnp.bfloat16
VMEM_BYTES = 12 * 1024 * 1024


def dot(a, b):
    return lax.dot_general(a, b, (((1,), (0,)), ((), ())), preferred_element_type=F32)


def dot_t(a, b):
    return lax.dot_general(a, b, (((1,), (1,)), ((), ())), preferred_element_type=F32)


def call(kernel, out_shape, inputs, scratch_shapes=(), smem=(), far=(), vmem=VMEM_BYTES, cost=0):
    def place(i):
        if i in far:
            return pl.BlockSpec(memory_space=pltpu.HBM)
        return pl.BlockSpec(memory_space=pltpu.SMEM if i in smem else pltpu.VMEM)

    return pl.pallas_call(
        kernel,
        out_shape=out_shape,
        in_specs=[place(i) for i in range(inputs)],
        out_specs=jax.tree.map(lambda _: pl.BlockSpec(memory_space=pltpu.VMEM), out_shape),
        scratch_shapes=list(scratch_shapes),
        compiler_params=pltpu.CompilerParams(vmem_limit_bytes=vmem),
        cost_estimate=pl.CostEstimate(flops=0, bytes_accessed=cost, transcendentals=0) if cost else None,
    )


def array(shape, dtype):
    return jax.ShapeDtypeStruct(shape, dtype)


def swapped(x, distance):
    return lax.ppermute(x, TREE, [(i, i ^ distance) for i in range(lax.axis_size(TREE))])


def by_core(x, distance_0, distance_1):
    pairs = []
    for i in range(lax.axis_size(TREE)):
        distance = distance_1 if i & 1 else distance_0
        if distance is not None:
            pairs.append((i, i ^ distance))
    return lax.ppermute(x, TREE, pairs)


def after(x, *others):
    return lax.optimization_barrier((x, *others))[0]


EXTRA = 16
FACTORS = 8
TOP = 14.0


def scaled_to(out_ref, values):
    rows, width = values.shape
    largest = jnp.max(jnp.max(jnp.abs(values), axis=0, keepdims=True), axis=1, keepdims=True)
    power = jnp.ceil(jnp.log2(jnp.maximum(largest, 1e-30))) - TOP
    power = jnp.clip(power, -112.0, 112.0)
    out_ref[:rows] = values * jnp.exp2(-power)
    row = lax.broadcasted_iota(jnp.int32, (EXTRA, width), 0).astype(F32)
    out_ref[rows:] = jnp.where(row < FACTORS, jnp.exp2(jnp.floor((power + row) / FACTORS)), 0.0)


def unscaled(packed):
    rows = packed.shape[0] - EXTRA
    values = packed[:rows].astype(F32)
    for factor in range(rows, rows + FACTORS):
        values = values * packed[factor : factor + 1].astype(F32)
    return values


def one_hot_of(order_ref, panels):
    local = lax.rem(order_ref[...], panels)
    rows = lax.broadcasted_iota(jnp.int32, (panels, panels), 0)
    return (rows == local).astype(F32).astype(BF16)


def signed_stack(x):
    half = x.shape[0] // 2
    real, imag = x[:half], x[half:]
    return jnp.concatenate(
        [jnp.concatenate([real, imag], axis=1), jnp.concatenate([imag, -real], axis=1)], axis=0
    )


def position():
    place = lax.axis_index(TREE)
    return place & 1, (place >> 1) & 1, (place >> 2) & 1


def first_kernel(
    tree_ref,
    basis_hbm,
    stack_ref,
    send_1_ref,
    keep_1_ref,
    part_2_ref,
    send_3_ref,
    keep_3_ref,
    basis,
    sems,
):
    core, _, low = position()
    levels, _, panels, rank = basis.shape
    half = rank // 2
    copies = [
        pltpu.make_async_copy(basis_hbm.at[level], basis.at[level], sems.at[level])
        for level in range(levels)
    ]
    for copy in copies:
        copy.start()
    stack = signed_stack(tree_ref[...])
    stack_ref[...] = stack

    def product(level, start, width):
        columns = basis[level, :, :, pl.ds(start, width)].reshape(2 * panels, width)
        return dot(stack, columns)

    copies[0].wait()
    send_1_ref[...] = product(0, pl.multiple_of((low ^ core ^ 1) * half, half), half)
    keep_1_ref[...] = product(0, pl.multiple_of((low ^ core) * half, half), half)
    copies[1].wait()
    part_2_ref[...] = product(1, 0, rank)
    copies[2].wait()
    send_3_ref[...] = product(2, pl.multiple_of((core ^ 1) * half, half), half)
    keep_3_ref[...] = product(2, pl.multiple_of(core * half, half), half)


def near_kernel(index_ref, stack_ref, near_ref, core_ref, far_ref, own_ref, sums):
    core, _, _ = position()
    _, block_count, neighbours, size, _ = near_ref.shape
    sums[...] = jnp.zeros_like(sums)
    base = index_ref[0, 0] - block_count
    for i in range(block_count):
        stack = jnp.concatenate(
            [stack_ref[:, j * size : (j + 1) * size] for j in (i, block_count + i)], axis=1
        )
        for k in range(0, neighbours, 2):
            pair = jnp.concatenate([near_ref[:, i, k], near_ref[:, i, k + 1]], axis=2)
            terms = dot(stack, pair.reshape(2 * size, 2 * size))
            for j in range(2):
                target = jnp.clip(index_ref[i, k + j] - base, 0, 3 * block_count - 1)
                sums[target] += terms[:, j * size : (j + 1) * size]
    for j in range(block_count):
        lanes = pl.ds(j * size, size)
        own_ref[:, lanes] = sums[block_count + j]
        far_ref[:, lanes] = sums[core * 2 * block_count + j].astype(BF16)
        core_ref[:, lanes] = sums[(1 - core) * 2 * block_count + j].astype(BF16)


def spread_kernel(keep_ref, got_ref, near_ref, far_ref):
    _, across, _ = position()
    width = near_ref.shape[1]
    for out, place in ((near_ref, across), (far_ref, across ^ 1)):
        lanes = pl.ds(pl.multiple_of(place * width, width), width)
        scaled_to(out, keep_ref[:, lanes] + got_ref[:, lanes])


def sums_kernel(part_2_ref, got_2_ref, keep_3_ref, got_3_ref, two_ref, three_ref):
    three_ref[...] = (keep_3_ref[...] + got_3_ref[...]).astype(BF16)
    scaled_to(two_ref, part_2_ref[...] + got_2_ref[...])


def expanded(coefficient, basis_ref, level, start, width):
    half = coefficient.shape[0] // 2
    turned = jnp.concatenate([-coefficient[half:], coefficient[:half]], axis=0)
    lanes = pl.ds(start, width)
    return dot_t(coefficient, basis_ref[level, 0, :, lanes]) + dot_t(
        turned, basis_ref[level, 1, :, lanes]
    )


def halo_kernel(own_ref, far_ref, three_ref, pair_ref, basis_ref, out_ref):
    core, _, _ = position()
    rows, half = three_ref.shape
    total = own_ref[...] + far_ref[...].astype(F32) + pair_ref[rows:].astype(F32)
    total += expanded(three_ref[...], basis_ref, 2, pl.multiple_of(core * half, half), half)
    total += expanded(pair_ref[:rows], basis_ref, 2, pl.multiple_of((1 - core) * half, half), half)
    out_ref[...] = total


def prepare_kernel(order_ref, basis_ref, forward_ref, moved_ref, ahead_ref, hot_ref):
    panels = hot_ref.shape[0]
    one_hot = one_hot_of(order_ref, panels)
    hot_ref[...] = one_hot
    for part in range(2):
        moved_ref[0, part] = dot(one_hot, basis_ref[0, part]).astype(BF16)
    ahead_ref[...] = forward_ref[...].reshape(ahead_ref.shape)


def second_kernel(hot_ref, base_ref, two_ref, basis_ref, ahead_ref, out_ref, grad_ref):
    total = base_ref[...] + expanded(two_ref[...], basis_ref, 1, 0, two_ref.shape[1])
    one_hot = hot_ref[...]
    field = jnp.zeros_like(total)
    for _ in range(3):
        piece = total.astype(BF16)
        total = total - piece.astype(F32)
        field += dot_t(piece, one_hot)
    out_ref[...] = field
    grad_ref[...] = jnp.sum(field * ahead_ref[...].astype(F32), axis=0, keepdims=True)


def last_kernel(
    base_ref, first_grad_ref, own_ref, mine_ref, got_ref, basis_ref, ahead_ref, field_ref, grad_ref, full
):
    core, across, low = position()
    both, width = own_ref.shape

    def put(flip, value):
        place = (2 * low + across) ^ flip
        full[:, pl.ds(pl.multiple_of(place * width, width), width)] = value

    put(0, own_ref[...])
    put(1, jnp.where(core == 0, mine_ref[:both], got_ref[:both]))
    put(2, jnp.where(core == 0, got_ref[:both], mine_ref[:both]))
    put(3, jnp.where(core == 0, got_ref[both:], mine_ref[both:]))
    two, rows, panels = field_ref.shape
    added = expanded(full[...], basis_ref, 0, 0, 4 * width)
    field_ref[...] = (base_ref[...] + added).reshape(two, rows, panels)
    total = first_grad_ref[...] + jnp.sum(added * ahead_ref[...].astype(F32), axis=0, keepdims=True)
    grad_ref[...] = -total / math.sqrt(rows)


def fast_body(sources, forward_field, row_bases, col_bases, near_blocks, near_index, cluster_order):
    two, rows, panels = sources.shape
    rank = row_bases.shape[3]
    both = two * rows
    half, quarter = rank // 2, rank // 4
    order = cluster_order.reshape(1, panels)
    halves = array((both, half), F32)
    one_hot = (lax.rem(cluster_order, panels)[None, :] == jnp.arange(panels)[:, None]).astype(BF16)
    tree = dot(sources.reshape(both, panels), one_hot).astype(BF16)
    stack, send_1, keep_1, part_2, send_3, keep_3 = call(
        first_kernel,
        (array((both, 2 * panels), BF16), halves, halves, array((both, rank), F32), halves, halves),
        2,
        scratch_shapes=[pltpu.VMEM((3, 2, panels, rank), BF16), pltpu.SemaphoreType.DMA((3,))],
        far=(1,),
        vmem=50 * 1024 * 1024,
    )(tree, row_bases)
    got_1 = swapped(send_1, 1)

    blocks = near_blocks.shape[1]
    size = near_blocks.shape[3]
    to_core, to_far, own = call(
        near_kernel,
        (array((both, panels), BF16), array((both, panels), BF16), array((both, panels), F32)),
        3,
        scratch_shapes=[pltpu.VMEM((3 * blocks, both, size), F32)],
        smem=(0,),
    )(near_index, stack, near_blocks)

    packed = array((both + EXTRA, quarter), F32)
    got_1, own, send_3, part_2 = lax.optimization_barrier((got_1, own, send_3, part_2))
    got_3 = swapped(send_3, 1)
    got_2 = swapped(part_2, 1)
    to_f, to_g = call(spread_kernel, (packed, packed), 2)(keep_1, got_1)
    got_f = by_core(to_f.astype(jnp.float16), 8, 12)
    got_g = by_core(to_g.astype(jnp.float16), 10, 14)

    two_sent, three_sent = call(
        sums_kernel, (array((both + EXTRA, rank), F32), array((both, half), BF16)), 4
    )(part_2, got_2, keep_3, after(got_3, to_f))
    mine_3 = swapped(three_sent, 2)
    two_sent = two_sent.astype(jnp.float16)
    got_cd = by_core(two_sent, 4, 6)
    peers = lax.axis_size(TREE)
    joints = [(i, i + 1) for i in range(1, peers - 1, 2)]
    far_halo = lax.ppermute(to_far, TREE, joints + [(b, a) for a, b in joints])

    got_f, got_g, _ = lax.optimization_barrier((got_f, got_g, two_sent))
    parts = lax.all_gather(unscaled(got_f) + unscaled(got_g), "rhs", axis=0)
    quarter_sum = (parts[0] + parts[1]).astype(BF16)
    got_a = by_core(quarter_sum, 2, 4)
    got_b = by_core(quarter_sum, None, 6)

    moved, ahead, hot = call(
        prepare_kernel,
        (
            array((1, 2, panels, rank), BF16),
            array((both, panels), BF16),
            array((panels, panels), BF16),
        ),
        3,
    )(after(order, quarter_sum), col_bases, forward_field)
    mine_3, own, _, _ = lax.optimization_barrier((mine_3, own, quarter_sum, moved))
    pair_3 = swapped(jnp.concatenate([mine_3, to_core], axis=0), 1)
    base = call(halo_kernel, array((both, panels), F32), 5)(own, far_halo, mine_3, pair_3, col_bases)
    got_cd = after(got_cd, quarter_sum)
    all_2 = (unscaled(got_cd) + unscaled(swapped(got_cd, 1))).astype(BF16)
    base, first_grad = call(
        second_kernel, (array((both, panels), F32), array((1, panels), F32)), 5
    )(hot, base, all_2, col_bases, ahead)
    mine_1 = jnp.concatenate([got_a, got_b], axis=0)
    field, grad = call(
        last_kernel,
        (array((two, rows, panels), F32), array((1, panels), F32)),
        7,
        scratch_shapes=[pltpu.VMEM((both, rank), BF16)],
    )(base, first_grad, quarter_sum, mine_1, swapped(mine_1, 1), moved, ahead)
    return field, grad.reshape(panels)


def conj_product(first_operand, second_operand, pattern):
    real_part = jnp.einsum(
        pattern, first_operand[0], second_operand[0], preferred_element_type=jnp.float32
    ) + jnp.einsum(pattern, first_operand[1], second_operand[1], preferred_element_type=jnp.float32)
    imag_part = jnp.einsum(
        pattern, first_operand[1], second_operand[0], preferred_element_type=jnp.float32
    ) - jnp.einsum(pattern, first_operand[0], second_operand[1], preferred_element_type=jnp.float32)
    return jnp.stack([real_part, imag_part])


def expand_basis(coefficient, col_basis):
    real_part = jnp.einsum(
        "rk,nk->rn", coefficient[0], col_basis[0], preferred_element_type=jnp.float32
    ) - jnp.einsum("rk,nk->rn", coefficient[1], col_basis[1], preferred_element_type=jnp.float32)
    imag_part = jnp.einsum(
        "rk,nk->rn", coefficient[0], col_basis[1], preferred_element_type=jnp.float32
    ) + jnp.einsum("rk,nk->rn", coefficient[1], col_basis[0], preferred_element_type=jnp.float32)
    return jnp.stack([real_part, imag_part])


def from_behind(x, by):
    peers = lax.axis_size(TREE)
    return lax.ppermute(x, TREE, [(i, i + by) for i in range(peers) if 0 <= i + by < peers])


def general_body(sources, forward_field, row_bases, col_bases, near_blocks, near_index, cluster_order):
    panel_count = sources.shape[2]
    columns = sources.shape[1]
    device = lax.axis_index(TREE)
    tree_bits = lax.axis_size(TREE).bit_length() - 1
    level_total = row_bases.shape[0]
    local_order = cluster_order - device * panel_count
    tree_sources = jnp.take(sources, local_order, axis=2)
    partials = [
        conj_product(tree_sources, row_bases[level_number], "rn,nk->rk")
        for level_number in range(level_total)
    ]
    block_count = near_blocks.shape[1]
    block_size = near_blocks.shape[3]
    targets = near_index - device * block_count + block_count
    one_hot = (
        targets[:, :, None] == jnp.arange(3 * block_count, dtype=jnp.int32)[None, None, :]
    ).astype(jnp.float32)
    block_sources = tree_sources.reshape(2, columns, block_count, block_size)
    terms = conj_product(block_sources, near_blocks, "rib,ikbc->rikc")
    buffer = jnp.einsum("zrikc,ikj->zrjc", terms, one_hot, precision=lax.Precision.HIGHEST)
    from_right = from_behind(buffer[:, :, :block_count], -1)
    from_left = from_behind(buffer[:, :, 2 * block_count :], 1)
    near_field = buffer[:, :, block_count : 2 * block_count] + from_right + from_left
    adjoint_tree = near_field.reshape(2, columns, panel_count)
    level_sums = []
    for level_number in range(level_total):
        running = partials[level_number]
        for bit_number in range(tree_bits - level_number - 1):
            running = running + swapped(running, 1 << bit_number)
        level_sums.append(running.astype(jnp.bfloat16))
    for level_number in range(level_total):
        sibling = swapped(level_sums[level_number], 1 << (tree_bits - level_number - 1))
        adjoint_tree = adjoint_tree + expand_basis(sibling, col_bases[level_number])
    adjoint_field = (
        jnp.zeros((2, columns, panel_count), jnp.float32).at[:, :, local_order].set(adjoint_tree)
    )
    forward_float = forward_field.astype(jnp.float32)
    gradient = -jnp.sum(adjoint_field * forward_float, axis=(0, 1)) / math.sqrt(columns)
    return (adjoint_field, gradient)


def body(*arrays):
    row_bases = arrays[2]
    fits = lax.axis_size("rhs") == 2 and lax.axis_size("leaf") == 8 and row_bases.shape[0] == 3
    return (fast_body if fits else general_body)(*arrays)


def solution(mesh):
    split = ("groups", "leaf", "rhs")
    in_specs = (
        P(None, None, split),
        P(None, None, split),
        P(None, None, split, None),
        P(None, None, split, None),
        P(None, split, None, None, None),
        P(split, None),
        P(split),
    )
    out_specs = (P(None, None, split), P(split))
    return jax.shard_map(body, mesh=mesh, in_specs=in_specs, out_specs=out_specs, check_vma=False)
```

```python
import math

import jax
import jax.numpy as jnp
from jax import lax
from jax.experimental import pallas as pl
from jax.experimental.pallas import tpu as pltpu
from jax.sharding import PartitionSpec as P

TREE = ("leaf", "rhs")
F32 = jnp.float32
BF16 = jnp.bfloat16
VMEM_BYTES = 12 * 1024 * 1024


def dot(a, b):
    return lax.dot_general(a, b, (((1,), (0,)), ((), ())), preferred_element_type=F32)


def dot_t(a, b):
    return lax.dot_general(a, b, (((1,), (1,)), ((), ())), preferred_element_type=F32)


def call(kernel, out_shape, inputs, scratch_shapes=(), smem=(), far=(), vmem=VMEM_BYTES, cost=0):
    def place(i):
        if i in far:
            return pl.BlockSpec(memory_space=pltpu.HBM)
        return pl.BlockSpec(memory_space=pltpu.SMEM if i in smem else pltpu.VMEM)

    return pl.pallas_call(
        kernel,
        out_shape=out_shape,
        in_specs=[place(i) for i in range(inputs)],
        out_specs=jax.tree.map(lambda _: pl.BlockSpec(memory_space=pltpu.VMEM), out_shape),
        scratch_shapes=list(scratch_shapes),
        compiler_params=pltpu.CompilerParams(vmem_limit_bytes=vmem),
        cost_estimate=pl.CostEstimate(flops=0, bytes_accessed=cost, transcendentals=0) if cost else None,
    )


def array(shape, dtype):
    return jax.ShapeDtypeStruct(shape, dtype)


def swapped(x, distance):
    return lax.ppermute(x, TREE, [(i, i ^ distance) for i in range(lax.axis_size(TREE))])


def by_core(x, distance_0, distance_1):
    pairs = []
    for i in range(lax.axis_size(TREE)):
        distance = distance_1 if i & 1 else distance_0
        if distance is not None:
            pairs.append((i, i ^ distance))
    return lax.ppermute(x, TREE, pairs)


def after(x, *others):
    return lax.optimization_barrier((x, *others))[0]


EXTRA = 16
FACTORS = 8
TOP = 14.0


def scaled_to(out_ref, values):
    rows, width = values.shape
    largest = jnp.max(jnp.max(jnp.abs(values), axis=0, keepdims=True), axis=1, keepdims=True)
    power = jnp.ceil(jnp.log2(jnp.maximum(largest, 1e-30))) - TOP
    power = jnp.clip(power, -112.0, 112.0)
    out_ref[:rows] = values * jnp.exp2(-power)
    row = lax.broadcasted_iota(jnp.int32, (EXTRA, width), 0).astype(F32)
    out_ref[rows:] = jnp.where(row < FACTORS, jnp.exp2(jnp.floor((power + row) / FACTORS)), 0.0)


def unscaled(packed):
    rows = packed.shape[0] - EXTRA
    values = packed[:rows].astype(F32)
    for factor in range(rows, rows + FACTORS):
        values = values * packed[factor : factor + 1].astype(F32)
    return values


def unscaled_in_kernel(ref):
    rows = ref.shape[0] - EXTRA
    scale = ref[rows : rows + 1]
    for factor in range(rows + 1, rows + FACTORS):
        scale = scale * ref[factor : factor + 1]
    return ref[:rows] * scale


def one_hot_of(order_ref, panels):
    local = lax.rem(order_ref[...], panels)
    rows = lax.broadcasted_iota(jnp.int32, (panels, panels), 0)
    return (rows == local).astype(F32).astype(BF16)


def signed_stack(x):
    half = x.shape[0] // 2
    real, imag = x[:half], x[half:]
    return jnp.concatenate(
        [jnp.concatenate([real, imag], axis=1), jnp.concatenate([imag, -real], axis=1)], axis=0
    )


def position():
    place = lax.axis_index(TREE)
    return place & 1, (place >> 1) & 1, (place >> 2) & 1


def product(stack, basis, i, start, width):
    panels = basis.shape[2]
    return dot(stack, basis[i, :, :, pl.ds(start, width)].reshape(2 * panels, width))


def first_kernel(tree_ref, basis_hbm, stack_ref, send_ref, keep_ref, basis, sems):
    core, _, low = position()
    half = basis.shape[3] // 2
    copy = pltpu.make_async_copy(basis_hbm.at[0], basis.at[0], sems.at[0])
    copy.start()
    stack = signed_stack(tree_ref[...])
    stack_ref[...] = stack
    copy.wait()
    send_ref[...] = product(stack, basis, 0, pl.multiple_of((low ^ core ^ 1) * half, half), half)
    keep_ref[...] = product(stack, basis, 0, pl.multiple_of((low ^ core) * half, half), half)


def others_kernel(stack_ref, basis_hbm, part_2_ref, send_3_ref, keep_3_ref, basis, sems):
    core, _, _ = position()
    rank = basis.shape[3]
    half = rank // 2
    copies = [
        pltpu.make_async_copy(basis_hbm.at[1 + i], basis.at[i], sems.at[i]) for i in range(2)
    ]
    for copy in copies:
        copy.start()
    stack = stack_ref[...]
    copies[0].wait()
    part_2_ref[...] = product(stack, basis, 0, 0, rank)
    copies[1].wait()
    send_3_ref[...] = product(stack, basis, 1, pl.multiple_of((core ^ 1) * half, half), half)
    keep_3_ref[...] = product(stack, basis, 1, pl.multiple_of(core * half, half), half)


def near_kernel(index_ref, stack_ref, near_ref, core_ref, far_ref, own_ref, sums):
    core, _, _ = position()
    _, block_count, neighbours, size, _ = near_ref.shape
    sums[...] = jnp.zeros_like(sums)
    base = index_ref[0, 0] - block_count
    for i in range(block_count):
        stack = jnp.concatenate(
            [stack_ref[:, j * size : (j + 1) * size] for j in (i, block_count + i)], axis=1
        )
        for k in range(0, neighbours, 2):
            pair = jnp.concatenate([near_ref[:, i, k], near_ref[:, i, k + 1]], axis=2)
            terms = dot(stack, pair.reshape(2 * size, 2 * size))
            for j in range(2):
                target = jnp.clip(index_ref[i, k + j] - base, 0, 3 * block_count - 1)
                sums[target] += terms[:, j * size : (j + 1) * size]
    for j in range(block_count):
        lanes = pl.ds(j * size, size)
        own_ref[:, lanes] = sums[block_count + j]
        far_ref[:, lanes] = sums[core * 2 * block_count + j].astype(BF16)
        core_ref[:, lanes] = sums[(1 - core) * 2 * block_count + j].astype(BF16)


def spread_kernel(keep_ref, got_ref, near_ref, far_ref):
    _, across, _ = position()
    width = near_ref.shape[1]
    for out, place in ((near_ref, across), (far_ref, across ^ 1)):
        lanes = pl.ds(pl.multiple_of(place * width, width), width)
        scaled_to(out, keep_ref[:, lanes] + got_ref[:, lanes])


def sums_kernel(part_2_ref, got_2_ref, keep_3_ref, got_3_ref, two_ref, *three_refs):
    for part, out in enumerate(three_refs):
        width = out.shape[1]
        lanes = pl.ds(part * width, width)
        out[...] = (keep_3_ref[:, lanes] + got_3_ref[:, lanes]).astype(BF16)
    scaled_to(two_ref, part_2_ref[...] + got_2_ref[...])


def expanded(coefficient, basis_ref, level, start, width):
    half = coefficient.shape[0] // 2
    turned = jnp.concatenate([-coefficient[half:], coefficient[:half]], axis=0)
    lanes = pl.ds(start, width)
    return dot_t(coefficient, basis_ref[level, 0, :, lanes]) + dot_t(
        turned, basis_ref[level, 1, :, lanes]
    )


def halo_kernel(own_ref, far_ref, three_ref, pair_ref, basis_ref, out_ref):
    core, _, _ = position()
    rows, half = three_ref.shape
    total = own_ref[...] + far_ref[...].astype(F32) + pair_ref[rows:].astype(F32)
    total += expanded(three_ref[...], basis_ref, 2, pl.multiple_of(core * half, half), half)
    total += expanded(pair_ref[:rows], basis_ref, 2, pl.multiple_of((1 - core) * half, half), half)
    out_ref[...] = total


def prepare_kernel(order_ref, basis_ref, forward_ref, moved_ref, ahead_ref, hot_ref):
    panels = hot_ref.shape[0]
    one_hot = one_hot_of(order_ref, panels)
    hot_ref[...] = one_hot
    for part in range(2):
        moved_ref[0, part] = dot(one_hot, basis_ref[0, part]).astype(BF16)
    ahead_ref[...] = forward_ref[...].reshape(ahead_ref.shape)


def second_kernel(
    hot_ref, base_ref, two_ref, two_got_ref, basis_ref, ahead_ref, out_ref, grad_ref
):
    two = (unscaled_in_kernel(two_ref) + unscaled_in_kernel(two_got_ref)).astype(BF16)
    total = base_ref[...] + expanded(two, basis_ref, 1, 0, two.shape[1])
    one_hot = hot_ref[...]
    field = jnp.zeros_like(total)
    for _ in range(2):
        piece = total.astype(BF16)
        total = total - piece.astype(F32)
        field += dot_t(piece, one_hot)
    out_ref[...] = field
    grad_ref[...] = jnp.sum(field * ahead_ref[...].astype(F32), axis=0, keepdims=True)


def last_kernel(
    base_ref, first_grad_ref, own_ref, mine_ref, got_ref, basis_ref, ahead_ref, field_ref, grad_ref, full
):
    core, across, low = position()
    both, width = own_ref.shape

    def put(flip, value):
        place = (2 * low + across) ^ flip
        full[:, pl.ds(pl.multiple_of(place * width, width), width)] = value

    put(0, own_ref[...])
    put(1, jnp.where(core == 0, mine_ref[:both], got_ref[:both]))
    put(2, jnp.where(core == 0, got_ref[:both], mine_ref[:both]))
    put(3, jnp.where(core == 0, got_ref[both:], mine_ref[both:]))
    two, rows, panels = field_ref.shape
    added = expanded(full[...], basis_ref, 0, 0, 4 * width)
    field_ref[...] = (base_ref[...] + added).reshape(two, rows, panels)
    total = first_grad_ref[...] + jnp.sum(added * ahead_ref[...].astype(F32), axis=0, keepdims=True)
    grad_ref[...] = -total / math.sqrt(rows)


def fast_body(sources, forward_field, row_bases, col_bases, near_blocks, near_index, cluster_order):
    two, rows, panels = sources.shape
    rank = row_bases.shape[3]
    both = two * rows
    half, quarter = rank // 2, rank // 4
    order = cluster_order.reshape(1, panels)
    halves = array((both, half), F32)
    one_hot = (lax.rem(cluster_order, panels)[None, :] == jnp.arange(panels)[:, None]).astype(BF16)
    tree = dot(sources.reshape(both, panels), one_hot).astype(BF16)
    stack, send_1, keep_1 = call(
        first_kernel,
        (array((both, 2 * panels), BF16), halves, halves),
        2,
        scratch_shapes=[pltpu.VMEM((1, 2, panels, rank), BF16), pltpu.SemaphoreType.DMA((1,))],
        far=(1,),
        vmem=52 * 1024 * 1024,
    )(tree, row_bases)
    got_1 = swapped(send_1, 1)
    part_2, send_3, keep_3 = call(
        others_kernel,
        (array((both, rank), F32), halves, halves),
        2,
        scratch_shapes=[pltpu.VMEM((2, 2, panels, rank), BF16), pltpu.SemaphoreType.DMA((2,))],
        far=(1,),
        vmem=50 * 1024 * 1024,
    )(stack, row_bases)

    got_1, send_3, part_2 = lax.optimization_barrier((got_1, send_3, part_2))
    got_3 = swapped(send_3, 1)
    got_2 = swapped(part_2, 1)
    packed = array((both + EXTRA, quarter), F32)
    to_f, to_g = call(spread_kernel, (packed, packed), 2)(keep_1, got_1)
    got_f = by_core(to_f.astype(jnp.float16), 8, 12)
    got_g = by_core(to_g.astype(jnp.float16), 10, 14)

    blocks = near_blocks.shape[1]
    size = near_blocks.shape[3]
    to_core, to_far, own = call(
        near_kernel,
        (array((both, panels), BF16), array((both, panels), BF16), array((both, panels), F32)),
        3,
        scratch_shapes=[pltpu.VMEM((3 * blocks, both, size), F32)],
        smem=(0,),
    )(near_index, after(stack, to_f), near_blocks)

    quarters = array((both, quarter), BF16)
    two_sent, *three_sent = call(
        sums_kernel, (array((both + EXTRA, rank), F32), quarters, quarters), 4
    )(part_2, got_2, keep_3, after(got_3, to_f))
    mine_3 = [swapped(part, 2) for part in three_sent]
    two_sent = two_sent.astype(jnp.float16)
    got_cd = by_core(two_sent, 4, 6)
    peers = lax.axis_size(TREE)
    joints = [(i, i + 1) for i in range(1, peers - 1, 2)]
    far_halo = lax.ppermute(to_far, TREE, joints + [(b, a) for a, b in joints])

    got_f, got_g, _, *mine_3 = lax.optimization_barrier((got_f, got_g, two_sent, *mine_3))
    middle = unscaled(got_f) + unscaled(got_g)
    parts = lax.all_gather(middle, "rhs", axis=0)
    quarter_sum = (parts[0] + parts[1]).astype(BF16)
    got_a = by_core(quarter_sum, 2, 4)
    got_b = by_core(quarter_sum, None, 6)

    moved, ahead, hot = call(
        prepare_kernel,
        (
            array((1, 2, panels, rank), BF16),
            array((both, panels), BF16),
            array((panels, panels), BF16),
        ),
        3,
    )(after(order, quarter_sum), col_bases, forward_field)
    mine_3 = jnp.concatenate(mine_3, axis=1)
    mine_3, own, _, _ = lax.optimization_barrier((mine_3, own, quarter_sum, moved))
    pair_3 = swapped(jnp.concatenate([mine_3, to_core], axis=0), 1)
    base = call(halo_kernel, array((both, panels), F32), 5)(own, far_halo, mine_3, pair_3, col_bases)
    got_cd = after(got_cd, quarter_sum)
    other_cd = swapped(got_cd, 1)
    base, first_grad = call(
        second_kernel, (array((both, panels), F32), array((1, panels), F32)), 6
    )(hot, base, got_cd.astype(F32), other_cd.astype(F32), col_bases, ahead)
    mine_1 = jnp.concatenate([got_a, got_b], axis=0)
    field, grad = call(
        last_kernel,
        (array((two, rows, panels), F32), array((1, panels), F32)),
        7,
        scratch_shapes=[pltpu.VMEM((both, rank), BF16)],
    )(base, first_grad, quarter_sum, mine_1, swapped(mine_1, 1), moved, ahead)
    return field, grad.reshape(panels)


def conj_product(first_operand, second_operand, pattern):
    real_part = jnp.einsum(
        pattern, first_operand[0], second_operand[0], preferred_element_type=jnp.float32
    ) + jnp.einsum(pattern, first_operand[1], second_operand[1], preferred_element_type=jnp.float32)
    imag_part = jnp.einsum(
        pattern, first_operand[1], second_operand[0], preferred_element_type=jnp.float32
    ) - jnp.einsum(pattern, first_operand[0], second_operand[1], preferred_element_type=jnp.float32)
    return jnp.stack([real_part, imag_part])


def expand_basis(coefficient, col_basis):
    real_part = jnp.einsum(
        "rk,nk->rn", coefficient[0], col_basis[0], preferred_element_type=jnp.float32
    ) - jnp.einsum("rk,nk->rn", coefficient[1], col_basis[1], preferred_element_type=jnp.float32)
    imag_part = jnp.einsum(
        "rk,nk->rn", coefficient[0], col_basis[1], preferred_element_type=jnp.float32
    ) + jnp.einsum("rk,nk->rn", coefficient[1], col_basis[0], preferred_element_type=jnp.float32)
    return jnp.stack([real_part, imag_part])


def from_behind(x, by):
    peers = lax.axis_size(TREE)
    return lax.ppermute(x, TREE, [(i, i + by) for i in range(peers) if 0 <= i + by < peers])


def general_body(sources, forward_field, row_bases, col_bases, near_blocks, near_index, cluster_order):
    panel_count = sources.shape[2]
    columns = sources.shape[1]
    device = lax.axis_index(TREE)
    tree_bits = lax.axis_size(TREE).bit_length() - 1
    level_total = row_bases.shape[0]
    local_order = cluster_order - device * panel_count
    tree_sources = jnp.take(sources, local_order, axis=2)
    partials = [
        conj_product(tree_sources, row_bases[level_number], "rn,nk->rk")
        for level_number in range(level_total)
    ]
    block_count = near_blocks.shape[1]
    block_size = near_blocks.shape[3]
    targets = near_index - device * block_count + block_count
    one_hot = (
        targets[:, :, None] == jnp.arange(3 * block_count, dtype=jnp.int32)[None, None, :]
    ).astype(jnp.float32)
    block_sources = tree_sources.reshape(2, columns, block_count, block_size)
    terms = conj_product(block_sources, near_blocks, "rib,ikbc->rikc")
    buffer = jnp.einsum("zrikc,ikj->zrjc", terms, one_hot, precision=lax.Precision.HIGHEST)
    from_right = from_behind(buffer[:, :, :block_count], -1)
    from_left = from_behind(buffer[:, :, 2 * block_count :], 1)
    near_field = buffer[:, :, block_count : 2 * block_count] + from_right + from_left
    adjoint_tree = near_field.reshape(2, columns, panel_count)
    level_sums = []
    for level_number in range(level_total):
        running = partials[level_number]
        for bit_number in range(tree_bits - level_number - 1):
            running = running + swapped(running, 1 << bit_number)
        level_sums.append(running.astype(jnp.bfloat16))
    for level_number in range(level_total):
        sibling = swapped(level_sums[level_number], 1 << (tree_bits - level_number - 1))
        adjoint_tree = adjoint_tree + expand_basis(sibling, col_bases[level_number])
    adjoint_field = (
        jnp.zeros((2, columns, panel_count), jnp.float32).at[:, :, local_order].set(adjoint_tree)
    )
    forward_float = forward_field.astype(jnp.float32)
    gradient = -jnp.sum(adjoint_field * forward_float, axis=(0, 1)) / math.sqrt(columns)
    return (adjoint_field, gradient)


def body(*arrays):
    row_bases = arrays[2]
    fits = lax.axis_size("rhs") == 2 and lax.axis_size("leaf") == 8 and row_bases.shape[0] == 3
    return (fast_body if fits else general_body)(*arrays)


def solution(mesh):
    split = ("groups", "leaf", "rhs")
    in_specs = (
        P(None, None, split),
        P(None, None, split),
        P(None, None, split, None),
        P(None, None, split, None),
        P(None, split, None, None, None),
        P(split, None),
        P(split),
    )
    out_specs = (P(None, None, split), P(split))
    return jax.shard_map(body, mesh=mesh, in_specs=in_specs, out_specs=out_specs, check_vma=False)
```

```python
import math

import jax
import jax.numpy as jnp
from jax import lax
from jax.experimental import pallas as pl
from jax.experimental.pallas import tpu as pltpu
from jax.sharding import PartitionSpec as P

TREE = ("leaf", "rhs")
F32 = jnp.float32
BF16 = jnp.bfloat16
VMEM_BYTES = 12 * 1024 * 1024


def dot(a, b):
    return lax.dot_general(a, b, (((1,), (0,)), ((), ())), preferred_element_type=F32)


def dot_t(a, b):
    return lax.dot_general(a, b, (((1,), (1,)), ((), ())), preferred_element_type=F32)


def call(kernel, out_shape, inputs, scratch_shapes=(), smem=(), far=(), vmem=VMEM_BYTES):
    def place(i):
        if i in far:
            return pl.BlockSpec(memory_space=pltpu.HBM)
        return pl.BlockSpec(memory_space=pltpu.SMEM if i in smem else pltpu.VMEM)

    return pl.pallas_call(
        kernel,
        out_shape=out_shape,
        in_specs=[place(i) for i in range(inputs)],
        out_specs=jax.tree.map(lambda _: pl.BlockSpec(memory_space=pltpu.VMEM), out_shape),
        scratch_shapes=list(scratch_shapes),
        compiler_params=pltpu.CompilerParams(vmem_limit_bytes=vmem),
    )


def array(shape, dtype):
    return jax.ShapeDtypeStruct(shape, dtype)


def swapped(x, distance):
    return lax.ppermute(x, TREE, [(i, i ^ distance) for i in range(lax.axis_size(TREE))])


def by_core(x, distance_0, distance_1):
    pairs = []
    for i in range(lax.axis_size(TREE)):
        distance = distance_1 if i & 1 else distance_0
        if distance is not None:
            pairs.append((i, i ^ distance))
    return lax.ppermute(x, TREE, pairs)


def after(x, *others):
    return lax.optimization_barrier((x, *others))[0]


EXTRA = 16
FACTORS = 8
TOP = 14.0


def scaled_to(out_ref, values):
    rows, width = values.shape
    largest = jnp.max(jnp.max(jnp.abs(values), axis=0, keepdims=True), axis=1, keepdims=True)
    power = jnp.ceil(jnp.log2(jnp.maximum(largest, 1e-30))) - TOP
    power = jnp.clip(power, -112.0, 112.0)
    out_ref[:rows] = values * jnp.exp2(-power)
    row = lax.broadcasted_iota(jnp.int32, (EXTRA, width), 0).astype(F32)
    out_ref[rows:] = jnp.where(row < FACTORS, jnp.exp2(jnp.floor((power + row) / FACTORS)), 0.0)


def unscaled(packed):
    rows = packed.shape[0] - EXTRA
    values = packed[:rows].astype(F32)
    for factor in range(rows, rows + FACTORS):
        values = values * packed[factor : factor + 1].astype(F32)
    return values


def unscaled_in_kernel(ref):
    rows = ref.shape[0] - EXTRA
    scale = ref[rows : rows + 1]
    for factor in range(rows + 1, rows + FACTORS):
        scale = scale * ref[factor : factor + 1]
    return ref[:rows] * scale


def one_hot_of(order_ref, panels):
    local = lax.rem(order_ref[...], panels)
    rows = lax.broadcasted_iota(jnp.int32, (panels, panels), 0)
    return (rows == local).astype(F32).astype(BF16)


def signed_stack(x):
    half = x.shape[0] // 2
    real, imag = x[:half], x[half:]
    return jnp.concatenate(
        [jnp.concatenate([real, imag], axis=1), jnp.concatenate([imag, -real], axis=1)], axis=0
    )


def position():
    place = lax.axis_index(TREE)
    return place & 1, (place >> 1) & 1, (place >> 2) & 1


def product(stack, basis, i, start, width):
    panels = basis.shape[2]
    return dot(stack, basis[i, :, :, pl.ds(start, width)].reshape(2 * panels, width))


def first_kernel(tree_ref, basis_hbm, stack_ref, send_ref, keep_ref, basis, sems):
    core, _, low = position()
    half = basis.shape[3] // 2
    copy = pltpu.make_async_copy(basis_hbm.at[0], basis.at[0], sems.at[0])
    copy.start()
    stack = signed_stack(tree_ref[...])
    stack_ref[...] = stack
    copy.wait()
    send_ref[...] = product(stack, basis, 0, pl.multiple_of((low ^ core ^ 1) * half, half), half)
    keep_ref[...] = product(stack, basis, 0, pl.multiple_of((low ^ core) * half, half), half)


def others_kernel(stack_ref, basis_hbm, send_ref, keep_3_ref, basis, sems):
    core, _, _ = position()
    rank = basis.shape[3]
    half = rank // 2
    copies = [
        pltpu.make_async_copy(basis_hbm.at[1 + i], basis.at[i], sems.at[i]) for i in range(2)
    ]
    for copy in copies:
        copy.start()
    stack = stack_ref[...]
    copies[0].wait()
    send_ref[:, :rank] = product(stack, basis, 0, 0, rank)
    copies[1].wait()
    send_ref[:, rank:] = product(stack, basis, 1, pl.multiple_of((core ^ 1) * half, half), half)
    keep_3_ref[...] = product(stack, basis, 1, pl.multiple_of(core * half, half), half)


def near_kernel(index_ref, stack_ref, near_ref, core_ref, far_ref, own_ref, sums):
    core, _, _ = position()
    _, block_count, neighbours, size, _ = near_ref.shape
    sums[...] = jnp.zeros_like(sums)
    base = index_ref[0, 0] - block_count
    for i in range(block_count):
        stack = jnp.concatenate(
            [stack_ref[:, j * size : (j + 1) * size] for j in (i, block_count + i)], axis=1
        )
        for k in range(0, neighbours, 2):
            pair = jnp.concatenate([near_ref[:, i, k], near_ref[:, i, k + 1]], axis=2)
            terms = dot(stack, pair.reshape(2 * size, 2 * size))
            for j in range(2):
                target = jnp.clip(index_ref[i, k + j] - base, 0, 3 * block_count - 1)
                sums[target] += terms[:, j * size : (j + 1) * size]
    for j in range(block_count):
        lanes = pl.ds(j * size, size)
        own_ref[:, lanes] = sums[block_count + j]
        far_ref[:, lanes] = sums[core * 2 * block_count + j].astype(BF16)
        core_ref[:, lanes] = sums[(1 - core) * 2 * block_count + j].astype(BF16)


def spread_kernel(keep_ref, got_ref, near_ref, far_ref):
    _, across, _ = position()
    width = near_ref.shape[1]
    for out, place in ((near_ref, across), (far_ref, across ^ 1)):
        lanes = pl.ds(pl.multiple_of(place * width, width), width)
        scaled_to(out, keep_ref[:, lanes] + got_ref[:, lanes])


def sums_kernel(sent_ref, got_ref, keep_3_ref, two_ref, *three_refs):
    rank = two_ref.shape[1]
    for part, out in enumerate(three_refs):
        width = out.shape[1]
        lanes, got_lanes = pl.ds(part * width, width), pl.ds(rank + part * width, width)
        out[...] = (keep_3_ref[:, lanes] + got_ref[:, got_lanes]).astype(BF16)
    scaled_to(two_ref, sent_ref[:, :rank] + got_ref[:, :rank])


def expanded(coefficient, basis_ref, level, start, width):
    half = coefficient.shape[0] // 2
    lanes = pl.ds(start, width)
    by_real = dot_t(coefficient, basis_ref[level, 0, :, lanes])
    by_imag = dot_t(coefficient, basis_ref[level, 1, :, lanes])
    return jnp.concatenate([by_real[:half] - by_imag[half:], by_imag[:half] + by_real[half:]], axis=0)


def prepare_kernel(order_ref, basis_ref, forward_ref, moved_ref, ahead_ref, hot_ref):
    panels = hot_ref.shape[0]
    one_hot = one_hot_of(order_ref, panels)
    hot_ref[...] = one_hot
    for part in range(2):
        moved_ref[0, part] = dot(one_hot, basis_ref[0, part]).astype(BF16)
    ahead_ref[...] = forward_ref[...].reshape(ahead_ref.shape)


def second_kernel(
    hot_ref,
    own_ref,
    far_ref,
    three_ref,
    pair_ref,
    two_ref,
    two_got_ref,
    basis_ref,
    ahead_ref,
    out_ref,
    grad_ref,
):
    core, _, _ = position()
    rows, half = three_ref.shape
    total = own_ref[...] + far_ref[...].astype(F32) + pair_ref[rows:].astype(F32)
    total += expanded(three_ref[...], basis_ref, 2, pl.multiple_of(core * half, half), half)
    total += expanded(pair_ref[:rows], basis_ref, 2, pl.multiple_of((1 - core) * half, half), half)
    two = (unscaled_in_kernel(two_ref) + unscaled_in_kernel(two_got_ref)).astype(BF16)
    total += expanded(two, basis_ref, 1, 0, two.shape[1])
    one_hot = hot_ref[...]
    field = jnp.zeros_like(total)
    for _ in range(2):
        piece = total.astype(BF16)
        total = total - piece.astype(F32)
        field += dot_t(piece, one_hot)
    out_ref[...] = field
    grad_ref[...] = jnp.sum(field * ahead_ref[...].astype(F32), axis=0, keepdims=True)


def last_kernel(
    base_ref, first_grad_ref, own_ref, mine_ref, got_ref, basis_ref, ahead_ref, field_ref, grad_ref, full
):
    core, across, low = position()
    both, width = own_ref.shape

    def put(flip, value):
        place = (2 * low + across) ^ flip
        full[:, pl.ds(pl.multiple_of(place * width, width), width)] = value

    put(0, own_ref[...])
    put(1, jnp.where(core == 0, mine_ref[:both], got_ref[:both]))
    put(2, jnp.where(core == 0, got_ref[:both], mine_ref[:both]))
    put(3, jnp.where(core == 0, got_ref[both:], mine_ref[both:]))
    two, rows, panels = field_ref.shape
    added = expanded(full[...], basis_ref, 0, 0, 4 * width)
    field_ref[...] = (base_ref[...] + added).reshape(two, rows, panels)
    total = first_grad_ref[...] + jnp.sum(added * ahead_ref[...].astype(F32), axis=0, keepdims=True)
    grad_ref[...] = -total / math.sqrt(rows)


def fast_body(sources, forward_field, row_bases, col_bases, near_blocks, near_index, cluster_order):
    two, rows, panels = sources.shape
    rank = row_bases.shape[3]
    both = two * rows
    half, quarter = rank // 2, rank // 4
    order = cluster_order.reshape(1, panels)
    halves = array((both, half), F32)
    one_hot = (lax.rem(cluster_order, panels)[None, :] == jnp.arange(panels)[:, None]).astype(BF16)
    tree = dot(sources.reshape(both, panels), one_hot).astype(BF16)
    stack, send_1, keep_1 = call(
        first_kernel,
        (array((both, 2 * panels), BF16), halves, halves),
        2,
        scratch_shapes=[pltpu.VMEM((1, 2, panels, rank), BF16), pltpu.SemaphoreType.DMA((1,))],
        far=(1,),
        vmem=52 * 1024 * 1024,
    )(tree, row_bases)
    got_1 = swapped(send_1, 1)
    send_23, keep_3 = call(
        others_kernel,
        (array((both, rank + half), F32), halves),
        2,
        scratch_shapes=[pltpu.VMEM((2, 2, panels, rank), BF16), pltpu.SemaphoreType.DMA((2,))],
        far=(1,),
        vmem=50 * 1024 * 1024,
    )(stack, row_bases)

    got_1, send_23 = lax.optimization_barrier((got_1, send_23))
    got_23 = swapped(send_23, 1)
    packed = array((both + EXTRA, quarter), F32)
    to_f, to_g = call(spread_kernel, (packed, packed), 2)(keep_1, got_1)
    got_f = by_core(to_f.astype(jnp.float16), 8, 12)
    got_g = by_core(to_g.astype(jnp.float16), 10, 14)

    quarters = array((both, quarter), BF16)
    two_sent, *three_sent = call(
        sums_kernel, (array((both + EXTRA, rank), F32), quarters, quarters), 3
    )(send_23, after(got_23, to_f), keep_3)
    mine_3 = [swapped(part, 2) for part in three_sent]
    two_sent = two_sent.astype(jnp.float16)
    got_cd = by_core(two_sent, 4, 6)
    blocks = near_blocks.shape[1]
    size = near_blocks.shape[3]
    to_core, to_far, own = call(
        near_kernel,
        (array((both, panels), BF16), array((both, panels), BF16), array((both, panels), F32)),
        3,
        scratch_shapes=[pltpu.VMEM((3 * blocks, both, size), F32)],
        smem=(0,),
    )(near_index, after(stack, two_sent), near_blocks)

    peers = lax.axis_size(TREE)
    joints = [(i, i + 1) for i in range(1, peers - 1, 2)]
    far_halo = lax.ppermute(to_far, TREE, joints + [(b, a) for a, b in joints])

    got_f, got_g, _, mine_3[0] = lax.optimization_barrier((got_f, got_g, two_sent, mine_3[0]))
    middle = unscaled(got_f) + unscaled(got_g)
    parts = lax.all_gather(middle, "rhs", axis=0)
    quarter_sum = (parts[0] + parts[1]).astype(BF16)
    got_a = by_core(quarter_sum, 2, 4)
    got_b = by_core(quarter_sum, None, 6)

    moved, ahead, hot = call(
        prepare_kernel,
        (
            array((1, 2, panels, rank), BF16),
            array((both, panels), BF16),
            array((panels, panels), BF16),
        ),
        3,
    )(after(order, quarter_sum), col_bases, forward_field)
    mine_3 = jnp.concatenate(mine_3, axis=1)
    mine_3, own, _, _ = lax.optimization_barrier((mine_3, own, quarter_sum, moved))
    pair_3 = swapped(jnp.concatenate([mine_3, to_core], axis=0), 1)
    got_cd = after(got_cd, quarter_sum)
    other_cd = swapped(got_cd, 1)
    base, first_grad = call(
        second_kernel, (array((both, panels), F32), array((1, panels), F32)), 9
    )(
        hot,
        own,
        far_halo,
        mine_3,
        pair_3,
        got_cd.astype(F32),
        other_cd.astype(F32),
        col_bases,
        ahead,
    )
    mine_1 = jnp.concatenate([got_a, got_b], axis=0)
    field, grad = call(
        last_kernel,
        (array((two, rows, panels), F32), array((1, panels), F32)),
        7,
        scratch_shapes=[pltpu.VMEM((both, rank), BF16)],
    )(base, first_grad, quarter_sum, mine_1, swapped(mine_1, 1), moved, ahead)
    return field, grad.reshape(panels)


def conj_product(first_operand, second_operand, pattern):
    real_part = jnp.einsum(
        pattern, first_operand[0], second_operand[0], preferred_element_type=jnp.float32
    ) + jnp.einsum(pattern, first_operand[1], second_operand[1], preferred_element_type=jnp.float32)
    imag_part = jnp.einsum(
        pattern, first_operand[1], second_operand[0], preferred_element_type=jnp.float32
    ) - jnp.einsum(pattern, first_operand[0], second_operand[1], preferred_element_type=jnp.float32)
    return jnp.stack([real_part, imag_part])


def expand_basis(coefficient, col_basis):
    real_part = jnp.einsum(
        "rk,nk->rn", coefficient[0], col_basis[0], preferred_element_type=jnp.float32
    ) - jnp.einsum("rk,nk->rn", coefficient[1], col_basis[1], preferred_element_type=jnp.float32)
    imag_part = jnp.einsum(
        "rk,nk->rn", coefficient[0], col_basis[1], preferred_element_type=jnp.float32
    ) + jnp.einsum("rk,nk->rn", coefficient[1], col_basis[0], preferred_element_type=jnp.float32)
    return jnp.stack([real_part, imag_part])


def from_behind(x, by):
    peers = lax.axis_size(TREE)
    return lax.ppermute(x, TREE, [(i, i + by) for i in range(peers) if 0 <= i + by < peers])


def general_body(sources, forward_field, row_bases, col_bases, near_blocks, near_index, cluster_order):
    panel_count = sources.shape[2]
    columns = sources.shape[1]
    device = lax.axis_index(TREE)
    tree_bits = lax.axis_size(TREE).bit_length() - 1
    level_total = row_bases.shape[0]
    local_order = cluster_order - device * panel_count
    tree_sources = jnp.take(sources, local_order, axis=2)
    partials = [
        conj_product(tree_sources, row_bases[level_number], "rn,nk->rk")
        for level_number in range(level_total)
    ]
    block_count = near_blocks.shape[1]
    block_size = near_blocks.shape[3]
    targets = near_index - device * block_count + block_count
    one_hot = (
        targets[:, :, None] == jnp.arange(3 * block_count, dtype=jnp.int32)[None, None, :]
    ).astype(jnp.float32)
    block_sources = tree_sources.reshape(2, columns, block_count, block_size)
    terms = conj_product(block_sources, near_blocks, "rib,ikbc->rikc")
    buffer = jnp.einsum("zrikc,ikj->zrjc", terms, one_hot, precision=lax.Precision.HIGHEST)
    from_right = from_behind(buffer[:, :, :block_count], -1)
    from_left = from_behind(buffer[:, :, 2 * block_count :], 1)
    near_field = buffer[:, :, block_count : 2 * block_count] + from_right + from_left
    adjoint_tree = near_field.reshape(2, columns, panel_count)
    level_sums = []
    for level_number in range(level_total):
        running = partials[level_number]
        for bit_number in range(tree_bits - level_number - 1):
            running = running + swapped(running, 1 << bit_number)
        level_sums.append(running.astype(jnp.bfloat16))
    for level_number in range(level_total):
        sibling = swapped(level_sums[level_number], 1 << (tree_bits - level_number - 1))
        adjoint_tree = adjoint_tree + expand_basis(sibling, col_bases[level_number])
    adjoint_field = (
        jnp.zeros((2, columns, panel_count), jnp.float32).at[:, :, local_order].set(adjoint_tree)
    )
    forward_float = forward_field.astype(jnp.float32)
    gradient = -jnp.sum(adjoint_field * forward_float, axis=(0, 1)) / math.sqrt(columns)
    return (adjoint_field, gradient)


def body(*arrays):
    row_bases = arrays[2]
    fits = lax.axis_size("rhs") == 2 and lax.axis_size("leaf") == 8 and row_bases.shape[0] == 3
    return (fast_body if fits else general_body)(*arrays)


def solution(mesh):
    split = ("groups", "leaf", "rhs")
    in_specs = (
        P(None, None, split),
        P(None, None, split),
        P(None, None, split, None),
        P(None, None, split, None),
        P(None, split, None, None, None),
        P(split, None),
        P(split),
    )
    out_specs = (P(None, None, split), P(split))
    return jax.shard_map(body, mesh=mesh, in_specs=in_specs, out_specs=out_specs, check_vma=False)
```

```python
import math

import jax
import jax.numpy as jnp
from jax import lax
from jax.experimental import pallas as pl
from jax.experimental.pallas import tpu as pltpu
from jax.sharding import PartitionSpec as P

TREE = ("leaf", "rhs")
F32 = jnp.float32
BF16 = jnp.bfloat16
VMEM_BYTES = 12 * 1024 * 1024


def dot(a, b):
    return lax.dot_general(a, b, (((1,), (0,)), ((), ())), preferred_element_type=F32)


def dot_t(a, b):
    return lax.dot_general(a, b, (((1,), (1,)), ((), ())), preferred_element_type=F32)


def call(kernel, out_shape, inputs, scratch_shapes=(), smem=(), far=(), vmem=VMEM_BYTES):
    def place(i):
        if i in far:
            return pl.BlockSpec(memory_space=pltpu.HBM)
        return pl.BlockSpec(memory_space=pltpu.SMEM if i in smem else pltpu.VMEM)

    return pl.pallas_call(
        kernel,
        out_shape=out_shape,
        in_specs=[place(i) for i in range(inputs)],
        out_specs=jax.tree.map(lambda _: pl.BlockSpec(memory_space=pltpu.VMEM), out_shape),
        scratch_shapes=list(scratch_shapes),
        compiler_params=pltpu.CompilerParams(vmem_limit_bytes=vmem),
    )


def array(shape, dtype):
    return jax.ShapeDtypeStruct(shape, dtype)


def swapped(x, distance):
    return lax.ppermute(x, TREE, [(i, i ^ distance) for i in range(lax.axis_size(TREE))])


def by_core(x, distance_0, distance_1):
    pairs = []
    for i in range(lax.axis_size(TREE)):
        distance = distance_1 if i & 1 else distance_0
        if distance is not None:
            pairs.append((i, i ^ distance))
    return lax.ppermute(x, TREE, pairs)


def after(x, *others):
    return lax.optimization_barrier((x, *others))[0]


EXTRA = 16
FACTORS = 8
TOP = 14.0


def scaled_to(out_ref, values):
    rows, width = values.shape
    largest = jnp.max(jnp.max(jnp.abs(values), axis=0, keepdims=True), axis=1, keepdims=True)
    power = jnp.ceil(jnp.log2(jnp.maximum(largest, 1e-30))) - TOP
    power = jnp.clip(power, -112.0, 112.0)
    out_ref[:rows] = values * jnp.exp2(-power)
    row = lax.broadcasted_iota(jnp.int32, (EXTRA, width), 0).astype(F32)
    out_ref[rows:] = jnp.where(row < FACTORS, jnp.exp2(jnp.floor((power + row) / FACTORS)), 0.0)


def unscaled(packed):
    rows = packed.shape[0] - EXTRA
    values = packed[:rows].astype(F32)
    for factor in range(rows, rows + FACTORS):
        values = values * packed[factor : factor + 1].astype(F32)
    return values


def unscaled_in_kernel(ref):
    rows = ref.shape[0] - EXTRA
    scale = ref[rows : rows + 1]
    for factor in range(rows + 1, rows + FACTORS):
        scale = scale * ref[factor : factor + 1]
    return ref[:rows] * scale


def one_hot_of(order_ref, panels):
    local = lax.rem(order_ref[...], panels)
    rows = lax.broadcasted_iota(jnp.int32, (panels, panels), 0)
    return (rows == local).astype(F32).astype(BF16)


def signed_stack(x):
    half = x.shape[0] // 2
    real, imag = x[:half], x[half:]
    return jnp.concatenate(
        [jnp.concatenate([real, imag], axis=1), jnp.concatenate([imag, -real], axis=1)], axis=0
    )


def position():
    place = lax.axis_index(TREE)
    return place & 1, (place >> 1) & 1, (place >> 2) & 1


def product(stack, basis, i, start, width):
    panels = basis.shape[2]
    return dot(stack, basis[i, :, :, pl.ds(start, width)].reshape(2 * panels, width))


def first_kernel(tree_ref, basis_hbm, stack_ref, send_ref, keep_ref, basis, sems):
    core, _, low = position()
    half = basis.shape[3] // 2
    copy = pltpu.make_async_copy(basis_hbm.at[0], basis.at[0], sems.at[0])
    copy.start()
    stack = signed_stack(tree_ref[...])
    stack_ref[...] = stack
    copy.wait()
    send_ref[...] = product(stack, basis, 0, pl.multiple_of((low ^ core ^ 1) * half, half), half)
    keep_ref[...] = product(stack, basis, 0, pl.multiple_of((low ^ core) * half, half), half)


def others_kernel(stack_ref, basis_hbm, send_ref, keep_3_ref, basis, sems):
    core, _, _ = position()
    rank = basis.shape[3]
    half = rank // 2
    copies = [
        pltpu.make_async_copy(basis_hbm.at[1 + i], basis.at[i], sems.at[i]) for i in range(2)
    ]
    for copy in copies:
        copy.start()
    stack = stack_ref[...]
    copies[0].wait()
    send_ref[:, :rank] = product(stack, basis, 0, 0, rank)
    copies[1].wait()
    send_ref[:, rank:] = product(stack, basis, 1, pl.multiple_of((core ^ 1) * half, half), half)
    keep_3_ref[...] = product(stack, basis, 1, pl.multiple_of(core * half, half), half)


def near_kernel(index_ref, stack_ref, near_ref, core_ref, far_ref, own_ref, sums):
    core, _, _ = position()
    _, block_count, neighbours, size, _ = near_ref.shape
    sums[...] = jnp.zeros_like(sums)
    base = index_ref[0, 0] - block_count
    for i in range(block_count):
        stack = jnp.concatenate(
            [stack_ref[:, j * size : (j + 1) * size] for j in (i, block_count + i)], axis=1
        )
        for k in range(0, neighbours, 4):
            four = jnp.concatenate([near_ref[:, i, k + j] for j in range(4)], axis=2)
            terms = dot(stack, four.reshape(2 * size, 4 * size))
            for j in range(4):
                target = jnp.clip(index_ref[i, k + j] - base, 0, 3 * block_count - 1)
                sums[target] += terms[:, j * size : (j + 1) * size]
    for j in range(block_count):
        lanes = pl.ds(j * size, size)
        own_ref[:, lanes] = sums[block_count + j]
        far_ref[:, lanes] = sums[core * 2 * block_count + j].astype(BF16)
        core_ref[:, lanes] = sums[(1 - core) * 2 * block_count + j].astype(BF16)


def spread_kernel(keep_ref, got_ref, near_ref, far_ref):
    _, across, _ = position()
    width = near_ref.shape[1]
    for out, place in ((near_ref, across), (far_ref, across ^ 1)):
        lanes = pl.ds(pl.multiple_of(place * width, width), width)
        scaled_to(out, keep_ref[:, lanes] + got_ref[:, lanes])


def sums_kernel(sent_ref, got_ref, keep_3_ref, two_ref, *three_refs):
    rank = two_ref.shape[1]
    for part, out in enumerate(three_refs):
        width = out.shape[1]
        lanes, got_lanes = pl.ds(part * width, width), pl.ds(rank + part * width, width)
        out[...] = (keep_3_ref[:, lanes] + got_ref[:, got_lanes]).astype(BF16)
    scaled_to(two_ref, sent_ref[:, :rank] + got_ref[:, :rank])


def expanded(coefficient, basis_ref, level, start, width):
    half = coefficient.shape[0] // 2
    lanes = pl.ds(start, width)
    by_real = dot_t(coefficient, basis_ref[level, 0, :, lanes])
    by_imag = dot_t(coefficient, basis_ref[level, 1, :, lanes])
    return jnp.concatenate([by_real[:half] - by_imag[half:], by_imag[:half] + by_real[half:]], axis=0)


def prepare_kernel(order_ref, basis_ref, forward_ref, moved_ref, ahead_ref, hot_ref):
    panels = hot_ref.shape[0]
    one_hot = one_hot_of(order_ref, panels)
    hot_ref[...] = one_hot
    for part in range(2):
        moved_ref[0, part] = dot(one_hot, basis_ref[0, part]).astype(BF16)
    ahead_ref[...] = forward_ref[...].reshape(ahead_ref.shape)


def second_kernel(
    hot_ref,
    own_ref,
    far_ref,
    three_ref,
    pair_ref,
    two_ref,
    two_got_ref,
    basis_ref,
    ahead_ref,
    out_ref,
    grad_ref,
):
    core, _, _ = position()
    rows, half = three_ref.shape
    total = own_ref[...] + far_ref[...].astype(F32) + pair_ref[rows:].astype(F32)
    total += expanded(three_ref[...], basis_ref, 2, pl.multiple_of(core * half, half), half)
    total += expanded(pair_ref[:rows], basis_ref, 2, pl.multiple_of((1 - core) * half, half), half)
    two = (unscaled_in_kernel(two_ref) + unscaled_in_kernel(two_got_ref)).astype(BF16)
    total += expanded(two, basis_ref, 1, 0, two.shape[1])
    one_hot = hot_ref[...]
    field = jnp.zeros_like(total)
    for _ in range(2):
        piece = total.astype(BF16)
        total = total - piece.astype(F32)
        field += dot_t(piece, one_hot)
    out_ref[...] = field
    grad_ref[...] = jnp.sum(field * ahead_ref[...].astype(F32), axis=0, keepdims=True)


def last_kernel(
    base_ref, first_grad_ref, own_ref, mine_ref, got_ref, basis_ref, ahead_ref, field_ref, grad_ref, full
):
    core, across, low = position()
    both, width = own_ref.shape

    def put(flip, value):
        place = (2 * low + across) ^ flip
        full[:, pl.ds(pl.multiple_of(place * width, width), width)] = value

    put(0, own_ref[...])
    put(1, jnp.where(core == 0, mine_ref[:both], got_ref[:both]))
    put(2, jnp.where(core == 0, got_ref[:both], mine_ref[:both]))
    put(3, jnp.where(core == 0, got_ref[both:], mine_ref[both:]))
    two, rows, panels = field_ref.shape
    added = expanded(full[...], basis_ref, 0, 0, 4 * width)
    field_ref[...] = (base_ref[...] + added).reshape(two, rows, panels)
    total = first_grad_ref[...] + jnp.sum(added * ahead_ref[...].astype(F32), axis=0, keepdims=True)
    grad_ref[...] = -total / math.sqrt(rows)


def fast_body(sources, forward_field, row_bases, col_bases, near_blocks, near_index, cluster_order):
    two, rows, panels = sources.shape
    rank = row_bases.shape[3]
    both = two * rows
    half, quarter = rank // 2, rank // 4
    order = cluster_order.reshape(1, panels)
    halves = array((both, half), F32)
    one_hot = (lax.rem(cluster_order, panels)[None, :] == jnp.arange(panels)[:, None]).astype(BF16)
    tree = dot(sources.reshape(both, panels), one_hot).astype(BF16)
    stack, send_1, keep_1 = call(
        first_kernel,
        (array((both, 2 * panels), BF16), halves, halves),
        2,
        scratch_shapes=[pltpu.VMEM((1, 2, panels, rank), BF16), pltpu.SemaphoreType.DMA((1,))],
        far=(1,),
        vmem=52 * 1024 * 1024,
    )(tree, row_bases)
    got_1 = swapped(send_1, 1)
    send_23, keep_3 = call(
        others_kernel,
        (array((both, rank + half), F32), halves),
        2,
        scratch_shapes=[pltpu.VMEM((2, 2, panels, rank), BF16), pltpu.SemaphoreType.DMA((2,))],
        far=(1,),
        vmem=50 * 1024 * 1024,
    )(stack, row_bases)

    got_1, send_23 = lax.optimization_barrier((got_1, send_23))
    got_23 = swapped(send_23, 1)
    packed = array((both + EXTRA, quarter), F32)
    to_f, to_g = call(spread_kernel, (packed, packed), 2)(keep_1, got_1)
    got_f = by_core(to_f.astype(jnp.float16), 8, 12)
    got_g = by_core(to_g.astype(jnp.float16), 10, 14)

    quarters = array((both, quarter), BF16)
    two_sent, *three_sent = call(
        sums_kernel, (array((both + EXTRA, rank), F32), quarters, quarters), 3
    )(send_23, after(got_23, to_f), keep_3)
    mine_3 = [swapped(part, 2) for part in three_sent]
    two_sent = two_sent.astype(jnp.float16)
    got_cd = by_core(two_sent, 4, 6)
    blocks = near_blocks.shape[1]
    size = near_blocks.shape[3]
    to_core, to_far, own = call(
        near_kernel,
        (array((both, panels), BF16), array((both, panels), BF16), array((both, panels), F32)),
        3,
        scratch_shapes=[pltpu.VMEM((3 * blocks, both, size), F32)],
        smem=(0,),
    )(near_index, after(stack, two_sent), near_blocks)

    peers = lax.axis_size(TREE)
    joints = [(i, i + 1) for i in range(1, peers - 1, 2)]
    far_halo = lax.ppermute(to_far, TREE, joints + [(b, a) for a, b in joints])

    got_f, got_g, _, mine_3[0] = lax.optimization_barrier((got_f, got_g, two_sent, mine_3[0]))
    middle = unscaled(got_f) + unscaled(got_g)
    parts = lax.all_gather(middle, "rhs", axis=0)
    quarter_sum = (parts[0] + parts[1]).astype(BF16)
    got_a = by_core(quarter_sum, 2, 4)
    got_b = by_core(quarter_sum, None, 6)

    moved, ahead, hot = call(
        prepare_kernel,
        (
            array((1, 2, panels, rank), BF16),
            array((both, panels), BF16),
            array((panels, panels), BF16),
        ),
        3,
    )(after(order, quarter_sum), col_bases, forward_field)
    mine_3 = jnp.concatenate(mine_3, axis=1)
    mine_3, own, _, _ = lax.optimization_barrier((mine_3, own, quarter_sum, moved))
    pair_3 = swapped(jnp.concatenate([mine_3, to_core], axis=0), 1)
    got_cd = after(got_cd, quarter_sum)
    other_cd = swapped(got_cd, 1)
    base, first_grad = call(
        second_kernel, (array((both, panels), F32), array((1, panels), F32)), 9
    )(
        hot,
        own,
        far_halo,
        mine_3,
        pair_3,
        got_cd.astype(F32),
        other_cd.astype(F32),
        col_bases,
        ahead,
    )
    mine_1 = jnp.concatenate([got_a, got_b], axis=0)
    field, grad = call(
        last_kernel,
        (array((two, rows, panels), F32), array((1, panels), F32)),
        7,
        scratch_shapes=[pltpu.VMEM((both, rank), BF16)],
    )(base, first_grad, quarter_sum, mine_1, swapped(mine_1, 1), moved, ahead)
    return field, grad.reshape(panels)


def conj_product(first_operand, second_operand, pattern):
    real_part = jnp.einsum(
        pattern, first_operand[0], second_operand[0], preferred_element_type=jnp.float32
    ) + jnp.einsum(pattern, first_operand[1], second_operand[1], preferred_element_type=jnp.float32)
    imag_part = jnp.einsum(
        pattern, first_operand[1], second_operand[0], preferred_element_type=jnp.float32
    ) - jnp.einsum(pattern, first_operand[0], second_operand[1], preferred_element_type=jnp.float32)
    return jnp.stack([real_part, imag_part])


def expand_basis(coefficient, col_basis):
    real_part = jnp.einsum(
        "rk,nk->rn", coefficient[0], col_basis[0], preferred_element_type=jnp.float32
    ) - jnp.einsum("rk,nk->rn", coefficient[1], col_basis[1], preferred_element_type=jnp.float32)
    imag_part = jnp.einsum(
        "rk,nk->rn", coefficient[0], col_basis[1], preferred_element_type=jnp.float32
    ) + jnp.einsum("rk,nk->rn", coefficient[1], col_basis[0], preferred_element_type=jnp.float32)
    return jnp.stack([real_part, imag_part])


def from_behind(x, by):
    peers = lax.axis_size(TREE)
    return lax.ppermute(x, TREE, [(i, i + by) for i in range(peers) if 0 <= i + by < peers])


def general_body(sources, forward_field, row_bases, col_bases, near_blocks, near_index, cluster_order):
    panel_count = sources.shape[2]
    columns = sources.shape[1]
    device = lax.axis_index(TREE)
    tree_bits = lax.axis_size(TREE).bit_length() - 1
    level_total = row_bases.shape[0]
    local_order = cluster_order - device * panel_count
    tree_sources = jnp.take(sources, local_order, axis=2)
    partials = [
        conj_product(tree_sources, row_bases[level_number], "rn,nk->rk")
        for level_number in range(level_total)
    ]
    block_count = near_blocks.shape[1]
    block_size = near_blocks.shape[3]
    targets = near_index - device * block_count + block_count
    one_hot = (
        targets[:, :, None] == jnp.arange(3 * block_count, dtype=jnp.int32)[None, None, :]
    ).astype(jnp.float32)
    block_sources = tree_sources.reshape(2, columns, block_count, block_size)
    terms = conj_product(block_sources, near_blocks, "rib,ikbc->rikc")
    buffer = jnp.einsum("zrikc,ikj->zrjc", terms, one_hot, precision=lax.Precision.HIGHEST)
    from_right = from_behind(buffer[:, :, :block_count], -1)
    from_left = from_behind(buffer[:, :, 2 * block_count :], 1)
    near_field = buffer[:, :, block_count : 2 * block_count] + from_right + from_left
    adjoint_tree = near_field.reshape(2, columns, panel_count)
    level_sums = []
    for level_number in range(level_total):
        running = partials[level_number]
        for bit_number in range(tree_bits - level_number - 1):
            running = running + swapped(running, 1 << bit_number)
        level_sums.append(running.astype(jnp.bfloat16))
    for level_number in range(level_total):
        sibling = swapped(level_sums[level_number], 1 << (tree_bits - level_number - 1))
        adjoint_tree = adjoint_tree + expand_basis(sibling, col_bases[level_number])
    adjoint_field = (
        jnp.zeros((2, columns, panel_count), jnp.float32).at[:, :, local_order].set(adjoint_tree)
    )
    forward_float = forward_field.astype(jnp.float32)
    gradient = -jnp.sum(adjoint_field * forward_float, axis=(0, 1)) / math.sqrt(columns)
    return (adjoint_field, gradient)


def body(*arrays):
    row_bases = arrays[2]
    fits = lax.axis_size("rhs") == 2 and lax.axis_size("leaf") == 8 and row_bases.shape[0] == 3
    return (fast_body if fits else general_body)(*arrays)


def solution(mesh):
    split = ("groups", "leaf", "rhs")
    in_specs = (
        P(None, None, split),
        P(None, None, split),
        P(None, None, split, None),
        P(None, None, split, None),
        P(None, split, None, None, None),
        P(split, None),
        P(split),
    )
    out_specs = (P(None, None, split), P(split))
    return jax.shard_map(body, mesh=mesh, in_specs=in_specs, out_specs=out_specs, check_vma=False)
```

```python
import math

import jax
import jax.numpy as jnp
from jax import lax
from jax.experimental import pallas as pl
from jax.experimental.pallas import tpu as pltpu
from jax.sharding import PartitionSpec as P

TREE = ("leaf", "rhs")
F32 = jnp.float32
BF16 = jnp.bfloat16
VMEM_BYTES = 12 * 1024 * 1024


def dot(a, b):
    return lax.dot_general(a, b, (((1,), (0,)), ((), ())), preferred_element_type=F32)


def dot_t(a, b):
    return lax.dot_general(a, b, (((1,), (1,)), ((), ())), preferred_element_type=F32)


def call(kernel, out_shape, inputs, scratch_shapes=(), smem=(), far=(), vmem=VMEM_BYTES):
    def place(i):
        if i in far:
            return pl.BlockSpec(memory_space=pltpu.HBM)
        return pl.BlockSpec(memory_space=pltpu.SMEM if i in smem else pltpu.VMEM)

    return pl.pallas_call(
        kernel,
        out_shape=out_shape,
        in_specs=[place(i) for i in range(inputs)],
        out_specs=jax.tree.map(lambda _: pl.BlockSpec(memory_space=pltpu.VMEM), out_shape),
        scratch_shapes=list(scratch_shapes),
        compiler_params=pltpu.CompilerParams(vmem_limit_bytes=vmem),
    )


def array(shape, dtype):
    return jax.ShapeDtypeStruct(shape, dtype)


def swapped(x, distance):
    return lax.ppermute(x, TREE, [(i, i ^ distance) for i in range(lax.axis_size(TREE))])


def by_core(x, distance_0, distance_1):
    pairs = []
    for i in range(lax.axis_size(TREE)):
        distance = distance_1 if i & 1 else distance_0
        if distance is not None:
            pairs.append((i, i ^ distance))
    return lax.ppermute(x, TREE, pairs)


def after(x, *others):
    return lax.optimization_barrier((x, *others))[0]


EXTRA = 16
FACTORS = 8
TOP = 14.0


def scaled_to(out_ref, values):
    rows, width = values.shape
    largest = jnp.max(jnp.max(jnp.abs(values), axis=0, keepdims=True), axis=1, keepdims=True)
    power = jnp.ceil(jnp.log2(jnp.maximum(largest, 1e-30))) - TOP
    power = jnp.clip(power, -112.0, 112.0)
    out_ref[:rows] = values * jnp.exp2(-power)
    row = lax.broadcasted_iota(jnp.int32, (EXTRA, width), 0).astype(F32)
    out_ref[rows:] = jnp.where(row < FACTORS, jnp.exp2(jnp.floor((power + row) / FACTORS)), 0.0)


def unscaled(packed):
    rows = packed.shape[0] - EXTRA
    values = packed[:rows].astype(F32)
    for factor in range(rows, rows + FACTORS):
        values = values * packed[factor : factor + 1].astype(F32)
    return values


def unscaled_in_kernel(ref):
    rows = ref.shape[0] - EXTRA
    scale = ref[rows : rows + 1]
    for factor in range(rows + 1, rows + FACTORS):
        scale = scale * ref[factor : factor + 1]
    return ref[:rows] * scale


def one_hot_of(order_ref, panels):
    local = lax.rem(order_ref[...], panels)
    rows = lax.broadcasted_iota(jnp.int32, (panels, panels), 0)
    return (rows == local).astype(F32).astype(BF16)


def signed_stack(x):
    half = x.shape[0] // 2
    real, imag = x[:half], x[half:]
    return jnp.concatenate(
        [jnp.concatenate([real, imag], axis=1), jnp.concatenate([imag, -real], axis=1)], axis=0
    )


def position():
    place = lax.axis_index(TREE)
    return place & 1, (place >> 1) & 1, (place >> 2) & 1


def product(stack, basis, i, start, width):
    panels = basis.shape[2]
    return dot(stack, basis[i, :, :, pl.ds(start, width)].reshape(2 * panels, width))


def first_kernel(tree_ref, basis_hbm, stack_ref, send_ref, keep_ref, basis, sems):
    core, _, low = position()
    half = basis.shape[3] // 2
    copy = pltpu.make_async_copy(basis_hbm.at[0], basis.at[0], sems.at[0])
    copy.start()
    stack = signed_stack(tree_ref[...])
    stack_ref[...] = stack
    copy.wait()
    send_ref[...] = product(stack, basis, 0, pl.multiple_of((low ^ core ^ 1) * half, half), half)
    keep_ref[...] = product(stack, basis, 0, pl.multiple_of((low ^ core) * half, half), half)


def others_kernel(stack_ref, basis_hbm, send_ref, keep_3_ref, basis, sems):
    core, _, _ = position()
    rank = basis.shape[3]
    half = rank // 2
    copies = [
        pltpu.make_async_copy(basis_hbm.at[1 + i], basis.at[i], sems.at[i]) for i in range(2)
    ]
    for copy in copies:
        copy.start()
    stack = stack_ref[...]
    copies[0].wait()
    send_ref[:, :rank] = product(stack, basis, 0, 0, rank)
    copies[1].wait()
    send_ref[:, rank:] = product(stack, basis, 1, pl.multiple_of((core ^ 1) * half, half), half)
    keep_3_ref[...] = product(stack, basis, 1, pl.multiple_of(core * half, half), half)


def near_kernel(index_ref, stack_ref, near_ref, core_ref, far_ref, own_ref, sums):
    core, _, _ = position()
    _, block_count, neighbours, size, _ = near_ref.shape
    sums[...] = jnp.zeros_like(sums)
    base = index_ref[0, 0] - block_count
    for i in range(block_count):
        stack = jnp.concatenate(
            [stack_ref[:, j * size : (j + 1) * size] for j in (i, block_count + i)], axis=1
        )
        for k in range(0, neighbours, 2):
            pair = jnp.concatenate([near_ref[:, i, k], near_ref[:, i, k + 1]], axis=2)
            terms = dot(stack, pair.reshape(2 * size, 2 * size))
            for j in range(2):
                target = jnp.clip(index_ref[i, k + j] - base, 0, 3 * block_count - 1)
                sums[target] += terms[:, j * size : (j + 1) * size]
    for j in range(block_count):
        lanes = pl.ds(j * size, size)
        own_ref[:, lanes] = sums[block_count + j]
        far_ref[:, lanes] = sums[core * 2 * block_count + j].astype(BF16)
        core_ref[:, lanes] = sums[(1 - core) * 2 * block_count + j].astype(BF16)


def spread_kernel(keep_ref, got_ref, near_ref, far_ref):
    _, across, _ = position()
    width = near_ref.shape[1]
    for out, place in ((near_ref, across), (far_ref, across ^ 1)):
        lanes = pl.ds(pl.multiple_of(place * width, width), width)
        scaled_to(out, keep_ref[:, lanes] + got_ref[:, lanes])


def sums_kernel(sent_ref, got_ref, keep_3_ref, two_ref, *three_refs):
    rank = two_ref.shape[1]
    for part, out in enumerate(three_refs):
        width = out.shape[1]
        lanes, got_lanes = pl.ds(part * width, width), pl.ds(rank + part * width, width)
        out[...] = (keep_3_ref[:, lanes] + got_ref[:, got_lanes]).astype(BF16)
    scaled_to(two_ref, sent_ref[:, :rank] + got_ref[:, :rank])


def expanded(coefficient, basis_ref, level, start, width):
    half = coefficient.shape[0] // 2
    lanes = pl.ds(start, width)
    by_real = dot_t(coefficient, basis_ref[level, 0, :, lanes])
    by_imag = dot_t(coefficient, basis_ref[level, 1, :, lanes])
    return jnp.concatenate([by_real[:half] - by_imag[half:], by_imag[:half] + by_real[half:]], axis=0)


def prepare_kernel(order_ref, basis_ref, forward_ref, moved_ref, ahead_ref, hot_ref):
    panels = hot_ref.shape[0]
    one_hot = one_hot_of(order_ref, panels)
    hot_ref[...] = one_hot
    for part in range(2):
        moved_ref[0, part] = dot(one_hot, basis_ref[0, part]).astype(BF16)
    ahead_ref[...] = forward_ref[...].reshape(ahead_ref.shape)


def second_kernel(
    hot_ref,
    own_ref,
    far_ref,
    three_ref,
    pair_ref,
    two_ref,
    two_got_ref,
    basis_ref,
    ahead_ref,
    out_ref,
    grad_ref,
):
    core, _, _ = position()
    rows, half = three_ref.shape
    total = own_ref[...] + far_ref[...].astype(F32) + pair_ref[rows:].astype(F32)
    total += expanded(three_ref[...], basis_ref, 2, pl.multiple_of(core * half, half), half)
    total += expanded(pair_ref[:rows], basis_ref, 2, pl.multiple_of((1 - core) * half, half), half)
    two = (unscaled_in_kernel(two_ref) + unscaled_in_kernel(two_got_ref)).astype(BF16)
    total += expanded(two, basis_ref, 1, 0, two.shape[1])
    one_hot = hot_ref[...]
    field = jnp.zeros_like(total)
    for _ in range(2):
        piece = total.astype(BF16)
        total = total - piece.astype(F32)
        field += dot_t(piece, one_hot)
    out_ref[...] = field
    grad_ref[...] = jnp.sum(field * ahead_ref[...].astype(F32), axis=0, keepdims=True)


def last_kernel(
    base_ref, first_grad_ref, own_ref, mine_ref, got_ref, basis_ref, ahead_ref, field_ref, grad_ref, full
):
    core, across, low = position()
    both, width = own_ref.shape

    def put(flip, value):
        place = (2 * low + across) ^ flip
        full[:, pl.ds(pl.multiple_of(place * width, width), width)] = value

    put(0, own_ref[...])
    put(1, jnp.where(core == 0, mine_ref[:both], got_ref[:both]))
    put(2, jnp.where(core == 0, got_ref[:both], mine_ref[:both]))
    put(3, jnp.where(core == 0, got_ref[both:], mine_ref[both:]))
    two, rows, panels = field_ref.shape
    added = expanded(full[...], basis_ref, 0, 0, 4 * width)
    field_ref[...] = (base_ref[...] + added).reshape(two, rows, panels)
    total = first_grad_ref[...] + jnp.sum(added * ahead_ref[...].astype(F32), axis=0, keepdims=True)
    grad_ref[...] = -total / math.sqrt(rows)


def fast_body(sources, forward_field, row_bases, col_bases, near_blocks, near_index, cluster_order):
    two, rows, panels = sources.shape
    rank = row_bases.shape[3]
    both = two * rows
    half, quarter = rank // 2, rank // 4
    order = cluster_order.reshape(1, panels)
    halves = array((both, half), F32)
    one_hot = (lax.rem(cluster_order, panels)[None, :] == jnp.arange(panels)[:, None]).astype(BF16)
    tree = dot(sources.reshape(both, panels), one_hot).astype(BF16)
    stack, send_1, keep_1 = call(
        first_kernel,
        (array((both, 2 * panels), BF16), halves, halves),
        2,
        scratch_shapes=[pltpu.VMEM((1, 2, panels, rank), BF16), pltpu.SemaphoreType.DMA((1,))],
        far=(1,),
        vmem=52 * 1024 * 1024,
    )(tree, row_bases)
    got_1 = swapped(send_1, 1)
    send_23, keep_3 = call(
        others_kernel,
        (array((both, rank + half), F32), halves),
        2,
        scratch_shapes=[pltpu.VMEM((2, 2, panels, rank), BF16), pltpu.SemaphoreType.DMA((2,))],
        far=(1,),
        vmem=50 * 1024 * 1024,
    )(stack, row_bases)

    got_1, send_23 = lax.optimization_barrier((got_1, send_23))
    got_23 = swapped(send_23, 1)
    packed = array((both + EXTRA, quarter), F32)
    to_f, to_g = call(spread_kernel, (packed, packed), 2)(keep_1, got_1)
    got_f = by_core(to_f.astype(jnp.float16), 8, 12)
    got_g = by_core(to_g.astype(jnp.float16), 10, 14)

    quarters = array((both, quarter), BF16)
    two_sent, *three_sent = call(
        sums_kernel, (array((both + EXTRA, rank), F32), quarters, quarters), 3
    )(send_23, after(got_23, to_f), keep_3)
    mine_3 = [swapped(part, 2) for part in three_sent]
    two_sent = two_sent.astype(jnp.float16)
    got_cd = by_core(two_sent, 4, 6)
    blocks = near_blocks.shape[1]
    size = near_blocks.shape[3]
    to_core, to_far, own = call(
        near_kernel,
        (array((both, panels), BF16), array((both, panels), BF16), array((both, panels), F32)),
        3,
        scratch_shapes=[pltpu.VMEM((3 * blocks, both, size), F32)],
        smem=(0,),
    )(near_index, after(stack, two_sent), near_blocks)

    peers = lax.axis_size(TREE)
    joints = [(i, i + 1) for i in range(1, peers - 1, 2)]
    far_halo = lax.ppermute(to_far, TREE, joints + [(b, a) for a, b in joints])

    got_f, got_g, _, mine_3[1] = lax.optimization_barrier((got_f, got_g, two_sent, mine_3[1]))
    middle = unscaled(got_f) + unscaled(got_g)
    parts = lax.all_gather(middle, "rhs", axis=0)
    quarter_sum = (parts[0] + parts[1]).astype(BF16)
    got_a = by_core(quarter_sum, 2, 4)
    got_b = by_core(quarter_sum, None, 6)

    moved, ahead, hot = call(
        prepare_kernel,
        (
            array((1, 2, panels, rank), BF16),
            array((both, panels), BF16),
            array((panels, panels), BF16),
        ),
        3,
    )(after(order, quarter_sum), col_bases, forward_field)
    mine_3 = jnp.concatenate(mine_3, axis=1)
    mine_3, own, _, _ = lax.optimization_barrier((mine_3, own, quarter_sum, moved))
    pair_3 = swapped(jnp.concatenate([mine_3, to_core], axis=0), 1)
    got_cd = after(got_cd, quarter_sum)
    other_cd = swapped(got_cd, 1)
    base, first_grad = call(
        second_kernel, (array((both, panels), F32), array((1, panels), F32)), 9
    )(
        hot,
        own,
        far_halo,
        mine_3,
        pair_3,
        got_cd.astype(F32),
        other_cd.astype(F32),
        col_bases,
        ahead,
    )
    mine_1 = jnp.concatenate([got_a, got_b], axis=0)
    field, grad = call(
        last_kernel,
        (array((two, rows, panels), F32), array((1, panels), F32)),
        7,
        scratch_shapes=[pltpu.VMEM((both, rank), BF16)],
    )(base, first_grad, quarter_sum, mine_1, swapped(mine_1, 1), moved, ahead)
    return field, grad.reshape(panels)


def conj_product(first_operand, second_operand, pattern):
    real_part = jnp.einsum(
        pattern, first_operand[0], second_operand[0], preferred_element_type=jnp.float32
    ) + jnp.einsum(pattern, first_operand[1], second_operand[1], preferred_element_type=jnp.float32)
    imag_part = jnp.einsum(
        pattern, first_operand[1], second_operand[0], preferred_element_type=jnp.float32
    ) - jnp.einsum(pattern, first_operand[0], second_operand[1], preferred_element_type=jnp.float32)
    return jnp.stack([real_part, imag_part])


def expand_basis(coefficient, col_basis):
    real_part = jnp.einsum(
        "rk,nk->rn", coefficient[0], col_basis[0], preferred_element_type=jnp.float32
    ) - jnp.einsum("rk,nk->rn", coefficient[1], col_basis[1], preferred_element_type=jnp.float32)
    imag_part = jnp.einsum(
        "rk,nk->rn", coefficient[0], col_basis[1], preferred_element_type=jnp.float32
    ) + jnp.einsum("rk,nk->rn", coefficient[1], col_basis[0], preferred_element_type=jnp.float32)
    return jnp.stack([real_part, imag_part])


def from_behind(x, by):
    peers = lax.axis_size(TREE)
    return lax.ppermute(x, TREE, [(i, i + by) for i in range(peers) if 0 <= i + by < peers])


def general_body(sources, forward_field, row_bases, col_bases, near_blocks, near_index, cluster_order):
    panel_count = sources.shape[2]
    columns = sources.shape[1]
    device = lax.axis_index(TREE)
    tree_bits = lax.axis_size(TREE).bit_length() - 1
    level_total = row_bases.shape[0]
    local_order = cluster_order - device * panel_count
    tree_sources = jnp.take(sources, local_order, axis=2)
    partials = [
        conj_product(tree_sources, row_bases[level_number], "rn,nk->rk")
        for level_number in range(level_total)
    ]
    block_count = near_blocks.shape[1]
    block_size = near_blocks.shape[3]
    targets = near_index - device * block_count + block_count
    one_hot = (
        targets[:, :, None] == jnp.arange(3 * block_count, dtype=jnp.int32)[None, None, :]
    ).astype(jnp.float32)
    block_sources = tree_sources.reshape(2, columns, block_count, block_size)
    terms = conj_product(block_sources, near_blocks, "rib,ikbc->rikc")
    buffer = jnp.einsum("zrikc,ikj->zrjc", terms, one_hot, precision=lax.Precision.HIGHEST)
    from_right = from_behind(buffer[:, :, :block_count], -1)
    from_left = from_behind(buffer[:, :, 2 * block_count :], 1)
    near_field = buffer[:, :, block_count : 2 * block_count] + from_right + from_left
    adjoint_tree = near_field.reshape(2, columns, panel_count)
    level_sums = []
    for level_number in range(level_total):
        running = partials[level_number]
        for bit_number in range(tree_bits - level_number - 1):
            running = running + swapped(running, 1 << bit_number)
        level_sums.append(running.astype(jnp.bfloat16))
    for level_number in range(level_total):
        sibling = swapped(level_sums[level_number], 1 << (tree_bits - level_number - 1))
        adjoint_tree = adjoint_tree + expand_basis(sibling, col_bases[level_number])
    adjoint_field = (
        jnp.zeros((2, columns, panel_count), jnp.float32).at[:, :, local_order].set(adjoint_tree)
    )
    forward_float = forward_field.astype(jnp.float32)
    gradient = -jnp.sum(adjoint_field * forward_float, axis=(0, 1)) / math.sqrt(columns)
    return (adjoint_field, gradient)


def body(*arrays):
    row_bases = arrays[2]
    fits = lax.axis_size("rhs") == 2 and lax.axis_size("leaf") == 8 and row_bases.shape[0] == 3
    return (fast_body if fits else general_body)(*arrays)


def solution(mesh):
    split = ("groups", "leaf", "rhs")
    in_specs = (
        P(None, None, split),
        P(None, None, split),
        P(None, None, split, None),
        P(None, None, split, None),
        P(None, split, None, None, None),
        P(split, None),
        P(split),
    )
    out_specs = (P(None, None, split), P(split))
    return jax.shard_map(body, mesh=mesh, in_specs=in_specs, out_specs=out_specs, check_vma=False)
```
